32 devices in a mesh: pipe: 4 (over z), zero: 8 (over y, x, core).
Axes of the slice: x: 2, y: 2, z: 4, core: 2. Of those that a mesh axis runs over, the one named last changes fastest.
Arguments:
- down_out: bfloat16 [4, 64, 2048], P('pipe', 'zero'), may hold values from -6 to 6
- up_out: bfloat16 [4, 64, 2048], P('pipe', 'zero'), may hold values from -6 to 6
- feeds: bfloat16 [2, 64, 2048], P(None, 'zero'), may hold values from -6 to 6
- order: int32 [2], replicated, may hold values from 0 to 1, each once
- gains: float32 [4, 2, 2048], P('pipe'), may hold values from 0.1 to 1.9
- gate_w: bfloat16 [4, 2, 2048, 4096], P('pipe', None, None, 'zero'), may hold values from -0.125 to 0.125
- up_w: bfloat16 [4, 2, 2048, 4096], P('pipe', None, None, 'zero'), may hold values from -0.125 to 0.125
- down_w: bfloat16 [4, 2, 4096, 2048], P('pipe', None, 'zero'), may hold values from -0.09375 to 0.09375
Outputs:
- down_next: bfloat16 [4, 64, 2048], P('pipe', 'zero')
- up_next: bfloat16 [4, 64, 2048], P('pipe', 'zero')
The draws below stay inside these ranges and needn't reach their ends.
Inputs may be any that keep to these rules, and one draw needn't show every extreme that they name: `order`: every micro-batch index enters exactly once.
All inputs are finite; a program needn't handle non-finite values.
Results may differ from the reference program's by a relative error of at most 0.02.
Values may be sent and summed in bfloat16 or wider, within the bound.
No kernel may reach another device: no remote copies, remote signals or barrier semaphores. Data moves between devices by JAX's collectives and lax.ppermute only.
A program may use at most 64 MiB of HBM per device.

```python
import jax
import jax.numpy as jnp
from jax import lax

D = 2048
FF = 4096
TICKS = 2
SECTIONS = 4
MB = 64
N_ZERO = 8


def steps_of(rng, dims, cuts, least, largest):
    loudness, own = 1.0, jax.random.fold_in(rng, 6)
    for position, parts in cuts:
        draws = jnp.exp(jax.random.uniform(jax.random.fold_in(own, position), (parts,), jnp.float32, least / len(cuts), largest / len(cuts)))
        loudness = loudness * jnp.repeat(draws, dims[position] // parts).reshape([-1 if axis == position else 1 for axis in range(len(dims))])
    return loudness


def normal_values(own_key, extent, spread, reach, cuts=(), held_as=jnp.bfloat16):
    drawn = jax.random.normal(own_key, extent, jnp.float32) * spread
    if len(cuts) > 0:
        drawn = steps_of(own_key, extent, cuts, -0.22, 0.18) * drawn
    return jnp.clip(drawn, min=-reach, max=reach).astype(held_as)


def setup_inputs(seed: int = 0) -> dict:
    splits = jax.random.split(jax.random.key(seed), 9)
    down_out = normal_values(splits[0], (SECTIONS, MB, D), 1.0, 6.0, ((0, 4), (1, 8)))
    up_out = normal_values(splits[1], (SECTIONS, MB, D), 1.0, 6.0, ((0, 4), (1, 8)))
    feeds = normal_values(splits[2], (TICKS, MB, D), 1.0, 6.0, ((1, 8),))
    order = jax.random.permutation(splits[3], TICKS).astype(jnp.int32)
    gains = jnp.clip(1.0 + 0.18 * jax.random.normal(splits[4], (SECTIONS, 2, D), jnp.float32), 0.1, 1.9)
    gate_w = normal_values(splits[5], (SECTIONS, 2, D, FF), D ** -0.5, 0.125, ((0, 4), (3, 8)))
    up_w = normal_values(splits[6], (SECTIONS, 2, D, FF), D ** -0.5, 0.125, ((0, 4), (3, 8)))
    down_w = normal_values(splits[7], (SECTIONS, 2, FF, D), FF ** -0.5, 0.09375, ((0, 4), (2, 8)))
    return dict(down_out=down_out, up_out=up_out, feeds=feeds, order=order, gains=gains, gate_w=gate_w, up_w=up_w, down_w=down_w)


def group(x, gain, w_gate, w_up, w_down):
    xf = x.astype(jnp.float32)
    normed = (xf * lax.rsqrt(lax.optimization_barrier(jnp.mean(xf * xf, axis=-1, keepdims=True)) + 1e-05) * gain).astype(jnp.bfloat16)
    gate = jnp.dot(normed, w_gate, preferred_element_type=jnp.float32)
    up = jnp.dot(normed, w_up, preferred_element_type=jnp.float32)
    hidden = (jax.nn.silu(gate) * up).astype(jnp.bfloat16)
    rows = hidden.shape[0]
    width = hidden.shape[1] // N_ZERO
    blocks = hidden.reshape(rows, N_ZERO, width).astype(jnp.float32)
    weights = w_down.reshape(N_ZERO, width, w_down.shape[1]).astype(jnp.float32)
    partial_value = jnp.einsum('mnf,nfd->nmd', blocks, weights).astype(jnp.bfloat16)
    summed = lax.optimization_barrier(jnp.sum(partial_value.astype(jnp.float32), axis=0))
    return (xf + summed).astype(jnp.bfloat16)

def section_pair(items):
    down_in, up_in, gain_pair, gate_pair, up_pair, down_pair = items
    first = group(down_in, gain_pair[0], gate_pair[0], up_pair[0], down_pair[0])
    second = group(up_in, gain_pair[1], gate_pair[1], up_pair[1], down_pair[1])
    return (first, second)

def reference(down_out, up_out, feeds, order, gains, gate_w, up_w, down_w):
    down_next = down_out
    up_next = up_out
    for tick in range(TICKS):
        entering = feeds[order[tick]]
        down_in = jnp.concatenate([entering[None], down_next[:-1]], axis=0)
        up_in = jnp.concatenate([up_next[1:], down_next[-1:]], axis=0)
        down_next, up_next = lax.map(section_pair, (down_in, up_in, gains, gate_w, up_w, down_w))
    return (down_next, up_next)
```

```python
import functools

import jax
import jax.numpy as jnp
from jax import lax
from jax.experimental import pallas as pl
from jax.experimental.pallas import tpu as pltpu
from jax.sharding import PartitionSpec as P

CORES = 2
EPS = 1e-05


def normalize(x, gain):
    xf = x.astype(jnp.float32)
    return (xf * lax.rsqrt(jnp.mean(xf * xf, axis=-1, keepdims=True) + EPS) * gain).astype(jnp.bfloat16)


def group_kernel(role_ref, mine_ref, sibling_ref, gains_ref, gate_ref, up_ref, down_ref, own_out, sibling_out):
    role = role_ref[0]
    for group, x_ref, out in ((1 - role, sibling_ref, sibling_out), (role, mine_ref, own_out)):
        normed = normalize(x_ref[...], gains_ref[pl.ds(group, 1), :])
        gate = jnp.dot(normed, gate_ref[group], preferred_element_type=jnp.float32)
        up = jnp.dot(normed, up_ref[group], preferred_element_type=jnp.float32)
        hidden = (gate / (1.0 + jnp.exp(-gate)) * up).astype(jnp.bfloat16)
        out[...] = jnp.dot(hidden, down_ref[group], preferred_element_type=jnp.float32).astype(out.dtype)


def groups(role, mine, sibling, gains, gate_w, up_w, down_w):
    vmem = pl.BlockSpec(memory_space=pltpu.VMEM)
    weights = gate_w.size + up_w.size + down_w.size
    return pl.pallas_call(
        group_kernel,
        out_shape=(
            jax.ShapeDtypeStruct(mine.shape, jnp.float32),
            jax.ShapeDtypeStruct(mine.shape, jnp.bfloat16),
        ),
        in_specs=[pl.BlockSpec(memory_space=pltpu.SMEM)] + [vmem] * 6,
        out_specs=(vmem, vmem),
        compiler_params=pltpu.CompilerParams(vmem_limit_bytes=20 * 2**20),
        cost_estimate=pl.CostEstimate(
            flops=2 * mine.shape[0] * weights, bytes_accessed=2 * weights, transcendentals=0
        ),
    )(role, mine, sibling, gains, gate_w, up_w, down_w)


def chip_pairs(chips, step):
    if chips & (chips - 1) == 0:
        return [(chip, chip ^ step) for chip in range(chips)]
    return [(chip, (chip + step) % chips) for chip in range(chips)]


def on_device(down_out, up_out, feeds, order, gains, gate_w, up_w, down_w):
    sections, zero = lax.axis_size("pipe"), lax.axis_size("zero")
    chips = zero // CORES
    section, place = lax.axis_index("pipe"), lax.axis_index("zero")
    core = place % CORES
    ticks = feeds.shape[0]
    both = ("pipe", "zero")

    def to_sibling(value):
        return lax.ppermute(value, "zero", [(k, k ^ 1) for k in range(zero)])

    def to_chip(value, step):
        pairs = [(a * CORES + r, b * CORES + r) for a, b in chip_pairs(chips, step) for r in range(CORES)]
        return lax.ppermute(value, "zero", pairs)

    def to_section(value, tick):
        pairs = []
        for s in range(sections):
            for k in range(zero):
                other = s - 1 if (s + k % CORES + tick) % 2 == 0 else s + 1
                other = other if 0 <= other < sections else s
                pairs.append((s * zero + k, other * zero + k))
        return lax.ppermute(value, both, pairs)

    def joined(own, other):
        first = jnp.where(core == 0, own, other)
        second = jnp.where(core == 0, other, own)
        return jnp.concatenate([first, second], axis=0)

    def role_at(tick):
        return (section + core + tick) % 2

    ascended = jnp.where(section == 0, feeds[order[0]], up_out[0])
    descended = down_out[0]
    rows = descended.shape[0]
    was_down = role_at(-1) == 0
    given = jnp.where(was_down, ascended, descended)
    later = [feeds[order[tick]] for tick in range(1, ticks)]
    taken = to_sibling(jnp.concatenate([given] + later, axis=0))
    state = joined(jnp.where(was_down, descended, ascended), taken[:rows])
    entering = [joined(own, taken[rows * (n + 1) : rows * (n + 2)]) for n, own in enumerate(later)]

    for tick in range(ticks):
        role = role_at(tick)
        if tick > 0:
            state = jnp.where((section == 0) & (role == 0), entering[tick - 1], state)
        x = to_section(state, tick)
        mine = jnp.concatenate([x] + [to_chip(x, step) for step in range(1, chips)], axis=0)
        sibling = to_sibling(mine)
        own_part, sibling_part = groups(
            role.reshape(1).astype(jnp.int32), mine, sibling, gains[0], gate_w[0], up_w[0], down_w[0]
        )
        part = own_part + to_sibling(sibling_part).astype(jnp.float32)
        height = x.shape[0]
        back = chips if chips & (chips - 1) == 0 else 0
        total = x.astype(jnp.float32) + part[:height]
        for step in range(1, chips):
            source = step if back else chips - step
            piece = part[source * height : (source + 1) * height].astype(jnp.bfloat16)
            total = total + to_chip(piece, step).astype(jnp.float32)
        state = total.astype(jnp.bfloat16)

    role = role_at(ticks - 1)
    kept = jnp.where(core == 0, state[:rows], state[rows:])
    received = to_sibling(jnp.where(core == 0, state[rows:], state[:rows]))
    down_state = jnp.where(role == 0, kept, received)
    up_state = jnp.where(role == 0, received, kept)
    return (down_state[None], up_state[None])


def solution(mesh):
    return jax.shard_map(
        on_device,
        mesh=mesh,
        in_specs=(
            P("pipe", "zero", None),
            P("pipe", "zero", None),
            P(None, "zero", None),
            P(),
            P("pipe", None, None),
            P("pipe", None, None, "zero"),
            P("pipe", None, None, "zero"),
            P("pipe", None, "zero", None),
        ),
        out_specs=(P("pipe", "zero", None), P("pipe", "zero", None)),
        check_vma=False,
    )
```

```python
import functools

import jax
import jax.numpy as jnp
from jax import lax
from jax.experimental import pallas as pl
from jax.experimental.pallas import tpu as pltpu
from jax.sharding import PartitionSpec as P

CORES = 2
EPS = 1e-05
LIMIT = 8 * 2**20
HOLD = (48 * 2**20, 44 * 2**20)
FLOPS = 2 * 10**10


def normalize(x, gain):
    xf = x.astype(jnp.float32)
    return (xf * lax.rsqrt(jnp.mean(xf * xf, axis=-1, keepdims=True) + EPS) * gain).astype(jnp.bfloat16)


def role_at(tick):
    return (lax.axis_index("pipe") + lax.axis_index("zero") % CORES + tick) % 2


def first_kernel(order_ref, down_hbm, up_hbm, feeds_hbm, own_out, given_out, down, up, feeds, sems):
    copies = [
        pltpu.make_async_copy(source, target, sems.at[n])
        for n, (source, target) in enumerate(((down_hbm, down), (up_hbm, up), (feeds_hbm, feeds)))
    ]
    for copy in copies:
        copy.start()
    for copy in copies:
        copy.wait()
    ticks = feeds.shape[0]

    def feed(tick):
        chosen = feeds[0].astype(jnp.float32)
        for n in range(1, ticks):
            chosen = jnp.where(order_ref[tick] == n, feeds[n].astype(jnp.float32), chosen)
        return chosen

    descended = down[0].astype(jnp.float32)
    ascended = jnp.where(lax.axis_index("pipe") == 0, feed(0), up[0].astype(jnp.float32))
    was_down = role_at(1) == 0
    own = jnp.where(was_down, descended, ascended)
    given = jnp.where(was_down, ascended, descended)
    later = [feed(tick) for tick in range(1, ticks)]
    own_out[...] = jnp.concatenate([own] + later, axis=0).astype(own_out.dtype)
    given_out[...] = jnp.concatenate([given] + later, axis=0).astype(given_out.dtype)


def first_rows(order, down_out, up_out, feeds):
    vmem, hbm = pl.BlockSpec(memory_space=pltpu.VMEM), pl.BlockSpec(memory_space=pltpu.HBM)
    ticks, rows, width = feeds.shape
    shape = jax.ShapeDtypeStruct((ticks * rows, width), feeds.dtype)
    return pl.pallas_call(
        first_kernel,
        out_shape=(shape, shape),
        in_specs=[pl.BlockSpec(memory_space=pltpu.SMEM), hbm, hbm, hbm],
        out_specs=(vmem, vmem),
        scratch_shapes=[pltpu.VMEM(a.shape, a.dtype) for a in (down_out, up_out, feeds)]
        + [pltpu.SemaphoreType.DMA((3,))],
        compiler_params=pltpu.CompilerParams(vmem_limit_bytes=4 * 2**20),
        cost_estimate=pl.CostEstimate(flops=FLOPS, bytes_accessed=8 * shape.size, transcendentals=0),
    )(order, down_out, up_out, feeds)


def group_kernel(tick, other, x_ref, gains_ref, gate_ref, up_ref, down_ref, out):
    group = (role_at(tick) + other) % 2
    normed = normalize(x_ref[...], gains_ref[pl.ds(group, 1), :])
    gate = jnp.dot(normed, gate_ref[group], preferred_element_type=jnp.float32)
    up = jnp.dot(normed, up_ref[group], preferred_element_type=jnp.float32)
    hidden = (gate / (1.0 + jnp.exp(-gate)) * up).astype(jnp.bfloat16)
    out[...] = jnp.dot(hidden, down_ref[group], preferred_element_type=jnp.float32).astype(out.dtype)


def held_kernel(count, x_ref, *refs):
    sources, x_out, outs, sems = refs[-2 * count - 2 : -count - 2], refs[-count - 2], refs[-count - 1 : -1], refs[-1]
    copies = [
        pltpu.make_async_copy(source.at[group], out.at[group], sems.at[n, group])
        for n, (source, out) in enumerate(zip(sources, outs))
        for group in range(source.shape[0])
    ]
    for copy in copies:
        copy.start()
    x_out[...] = x_ref[...]
    for copy in copies:
        copy.wait()


def held(x, weights, after=()):
    vmem = pl.BlockSpec(memory_space=pltpu.VMEM)
    results = (x,) + tuple(weights)
    return pl.pallas_call(
        functools.partial(held_kernel, len(weights)),
        out_shape=tuple(jax.ShapeDtypeStruct(a.shape, a.dtype) for a in results),
        in_specs=[vmem] * (1 + len(after)) + [pl.BlockSpec(memory_space=pl.ANY)] * len(weights),
        out_specs=(vmem,) * len(results),
        scratch_shapes=[pltpu.SemaphoreType.DMA((len(weights), weights[0].shape[0]))],
        compiler_params=pltpu.CompilerParams(vmem_limit_bytes=HOLD[len(weights) - 1]),
        cost_estimate=pl.CostEstimate(flops=FLOPS // 8, bytes_accessed=0, transcendentals=0),
    )(x, *after, *weights)


def stack_kernel(*refs):
    height = refs[0].shape[0]
    for slot, ref in enumerate(refs[:-1]):
        refs[-1][slot * height : (slot + 1) * height] = ref[...]


def stacked(pieces):
    vmem = pl.BlockSpec(memory_space=pltpu.VMEM)
    rows, width = pieces[0].shape
    return pl.pallas_call(
        stack_kernel,
        out_shape=jax.ShapeDtypeStruct((len(pieces) * rows, width), pieces[0].dtype),
        in_specs=[vmem] * len(pieces),
        out_specs=vmem,
        compiler_params=pltpu.CompilerParams(vmem_limit_bytes=LIMIT),
    )(*pieces)


def partial(tick, other, x, gains, weights):
    vmem = pl.BlockSpec(memory_space=pltpu.VMEM)
    size = sum(w.size // w.shape[0] for w in weights)
    return pl.pallas_call(
        functools.partial(group_kernel, tick, other),
        out_shape=jax.ShapeDtypeStruct(x.shape, jnp.bfloat16 if other else jnp.float32),
        in_specs=[vmem] * (2 + len(weights)),
        out_specs=vmem,
        compiler_params=pltpu.CompilerParams(vmem_limit_bytes=LIMIT),
        cost_estimate=pl.CostEstimate(flops=2 * x.shape[0] * size, bytes_accessed=2 * size, transcendentals=0),
    )(x, gains, *weights)


def chip_pairs(chips, step):
    if chips & (chips - 1) == 0:
        return [(chip, chip ^ step) for chip in range(chips)]
    return [(chip, (chip + step) % chips) for chip in range(chips)]


def on_device(down_out, up_out, feeds, order, gains, gate_w, up_w, down_w):
    sections, zero = lax.axis_size("pipe"), lax.axis_size("zero")
    chips = zero // CORES
    section, place = lax.axis_index("pipe"), lax.axis_index("zero")
    core = place % CORES
    ticks = feeds.shape[0]
    both = ("pipe", "zero")

    def to_sibling(value):
        return lax.ppermute(value, "zero", [(k, k ^ 1) for k in range(zero)])

    def to_chip(value, step):
        pairs = [(a * CORES + r, b * CORES + r) for a, b in chip_pairs(chips, step) for r in range(CORES)]
        return lax.ppermute(value, "zero", pairs)

    def to_section(value, tick):
        pairs = []
        for s in range(sections):
            for k in range(zero):
                other = s - 1 if (s + k % CORES + tick) % 2 == 0 else s + 1
                other = other if 0 <= other < sections else s
                pairs.append((s * zero + k, other * zero + k))
        return lax.ppermute(value, both, pairs)

    def joined(own, other):
        first = jnp.where(core == 0, own, other)
        second = jnp.where(core == 0, other, own)
        return jnp.concatenate([first, second], axis=0)

    own, given = first_rows(order, down_out, up_out, feeds)
    rows = down_out.shape[1]
    taken = to_sibling(given)
    state, *entering = [
        joined(own[n * rows : (n + 1) * rows], taken[n * rows : (n + 1) * rows]) for n in range(ticks)
    ]

    for tick in range(ticks):
        if tick > 0:
            state = jnp.where((section == 0) & (role_at(tick) == 0), entering[tick - 1], state)
        mark, gate = held(state, [gate_w[0]])
        x = to_section(state, tick)
        own, up, down = held(x, [up_w[0], down_w[0]], [mark])
        weights = (gate, up, down)
        pieces = [own] + [to_chip(x, step) for step in range(1, chips)]
        mine = stacked(pieces)
        sibling = to_sibling(mine)
        part = partial(tick, 0, mine, gains[0], weights)
        given = partial(tick, 1, sibling, gains[0], weights)
        part = part + to_sibling(given).astype(jnp.float32)
        height = x.shape[0]
        total = x.astype(jnp.float32) + part[:height]
        for step in range(1, chips):
            slot = step if chips & (chips - 1) == 0 else chips - step
            piece = part[slot * height : (slot + 1) * height].astype(jnp.bfloat16)
            total = total + to_chip(piece, step).astype(jnp.float32)
        state = total.astype(jnp.bfloat16)

    role = role_at(ticks - 1)
    kept = jnp.where(core == 0, state[:rows], state[rows:])
    received = to_sibling(jnp.where(core == 0, state[rows:], state[:rows]))
    down_state = jnp.where(role == 0, kept, received)
    up_state = jnp.where(role == 0, received, kept)
    return (down_state[None], up_state[None])


def solution(mesh):
    return jax.shard_map(
        on_device,
        mesh=mesh,
        in_specs=(
            P("pipe", "zero", None),
            P("pipe", "zero", None),
            P(None, "zero", None),
            P(),
            P("pipe", None, None),
            P("pipe", None, None, "zero"),
            P("pipe", None, None, "zero"),
            P("pipe", None, "zero", None),
        ),
        out_specs=(P("pipe", "zero", None), P("pipe", "zero", None)),
        check_vma=False,
    )
```

```python
import functools

import jax
import jax.numpy as jnp
from jax import lax
from jax.experimental import pallas as pl
from jax.experimental.pallas import tpu as pltpu
from jax.sharding import PartitionSpec as P

CORES = 2
EPS = 1e-05
LIMIT = 8 * 2**20
BESIDE = 10**10


def normalize(x, gain):
    xf = x.astype(jnp.float32)
    return (xf * lax.rsqrt(jnp.mean(xf * xf, axis=-1, keepdims=True) + EPS) * gain).astype(jnp.bfloat16)


def role_at(tick):
    return (lax.axis_index("pipe") + lax.axis_index("zero") % CORES + tick) % 2


def group_kernel(tick, other, x_ref, gains_ref, gate_ref, up_ref, down_ref, out):
    group = (role_at(tick) + other) % 2
    normed = normalize(x_ref[...], gains_ref[pl.ds(group, 1), :])
    gate = jnp.dot(normed, gate_ref[group], preferred_element_type=jnp.float32)
    up = jnp.dot(normed, up_ref[group], preferred_element_type=jnp.float32)
    hidden = (gate / (1.0 + jnp.exp(-gate)) * up).astype(jnp.bfloat16)
    out[...] = jnp.dot(hidden, down_ref[group], preferred_element_type=jnp.float32).astype(out.dtype)


def pass_kernel(x_ref, out):
    out[...] = x_ref[...]


def passed(x):
    vmem = pl.BlockSpec(memory_space=pltpu.VMEM)
    return pl.pallas_call(
        pass_kernel,
        out_shape=jax.ShapeDtypeStruct(x.shape, x.dtype),
        in_specs=[vmem],
        out_specs=vmem,
        compiler_params=pltpu.CompilerParams(vmem_limit_bytes=LIMIT),
        cost_estimate=pl.CostEstimate(flops=BESIDE, bytes_accessed=4 * x.size, transcendentals=0),
    )(x)


def stack_kernel(mark_ref, *refs):
    height = refs[0].shape[0]
    for slot, ref in enumerate(refs[:-1]):
        refs[-1][slot * height : (slot + 1) * height] = ref[...]


def stacked(pieces, mark):
    vmem = pl.BlockSpec(memory_space=pltpu.VMEM)
    rows, width = mark.shape
    return pl.pallas_call(
        stack_kernel,
        out_shape=jax.ShapeDtypeStruct((len(pieces) * rows, width), mark.dtype),
        in_specs=[vmem] * (1 + len(pieces)),
        out_specs=vmem,
        compiler_params=pltpu.CompilerParams(vmem_limit_bytes=LIMIT),
    )(mark, *pieces)


def sum_kernel(*refs):
    total = refs[0][...].astype(jnp.float32)
    for ref in refs[1:-1]:
        total += ref[...].astype(jnp.float32)
    refs[-1][...] = total.astype(refs[-1].dtype)


def summed(parts):
    vmem = pl.BlockSpec(memory_space=pltpu.VMEM)
    return pl.pallas_call(
        sum_kernel,
        out_shape=jax.ShapeDtypeStruct(parts[0].shape, jnp.bfloat16),
        in_specs=[vmem] * len(parts),
        out_specs=vmem,
        compiler_params=pltpu.CompilerParams(vmem_limit_bytes=LIMIT),
    )(*parts)


def partial(tick, other, x, gains, weights):
    vmem = pl.BlockSpec(memory_space=pltpu.VMEM)
    size = sum(w.size // w.shape[0] for w in weights)
    return pl.pallas_call(
        functools.partial(group_kernel, tick, other),
        out_shape=jax.ShapeDtypeStruct(x.shape, jnp.bfloat16 if other else jnp.float32),
        in_specs=[vmem] * (2 + len(weights)),
        out_specs=vmem,
        compiler_params=pltpu.CompilerParams(vmem_limit_bytes=LIMIT),
        cost_estimate=pl.CostEstimate(flops=2 * x.shape[0] * size, bytes_accessed=2 * size, transcendentals=0),
    )(x, gains, *weights)


def chip_pairs(chips, step):
    if chips & (chips - 1) == 0:
        return [(chip, chip ^ step) for chip in range(chips)]
    return [(chip, (chip + step) % chips) for chip in range(chips)]


def on_device(down_out, up_out, feeds, order, gains, gate_w, up_w, down_w):
    sections, zero = lax.axis_size("pipe"), lax.axis_size("zero")
    chips = zero // CORES
    section, place = lax.axis_index("pipe"), lax.axis_index("zero")
    core = place % CORES
    ticks = feeds.shape[0]
    both = ("pipe", "zero")

    def to_sibling(value):
        return lax.ppermute(value, "zero", [(k, k ^ 1) for k in range(zero)])

    def to_chip(value, step):
        pairs = [(a * CORES + r, b * CORES + r) for a, b in chip_pairs(chips, step) for r in range(CORES)]
        return lax.ppermute(value, "zero", pairs)

    def to_next(value, tick, step):
        pairs = []
        for s in range(sections):
            for r in range(CORES):
                other = s - 1 if (s + r + tick) % 2 == 0 else s + 1
                other = other if 0 <= other < sections else s
                for a, b in chip_pairs(chips, step):
                    pairs.append((s * zero + a * CORES + r, other * zero + b * CORES + r))
        return lax.ppermute(value, both, pairs)

    def joined(own, other):
        first = jnp.where(core == 0, own, other)
        second = jnp.where(core == 0, other, own)
        return jnp.concatenate([first, second], axis=0)

    weights = (gate_w[0], up_w[0], down_w[0])
    chosen = (order[:, None] == jnp.arange(ticks)[None, :]).astype(feeds.dtype)
    fed = jnp.einsum("tn,nrd->trd", chosen, feeds, preferred_element_type=jnp.float32).astype(feeds.dtype)
    was_down = role_at(1) == 0
    ascended = jnp.where(section == 0, fed[0], up_out[0])
    given = jnp.where(was_down, ascended, down_out[0])
    own = jnp.where(was_down, down_out[0], ascended)
    rows = own.shape[0]
    given = jnp.concatenate([given] + [fed[tick] for tick in range(1, ticks)], axis=0)
    own, given = lax.optimization_barrier((own, given))
    taken = to_sibling(given)
    state = joined(own, taken[:rows])
    entering = [joined(given[rows * tick : rows * (tick + 1)], taken[rows * tick : rows * (tick + 1)]) for tick in range(1, ticks)]

    for tick in range(ticks):
        if tick == 0:
            pieces = [to_next(state, tick, step) for step in range(chips)]
        else:
            pieces = [state] + [to_chip(state, step) for step in range(1, chips)]
        x = pieces[0]
        height = x.shape[0]
        mine = stacked(pieces, passed(state))
        sibling = to_sibling(mine)
        part = partial(tick, 0, mine, gains[0], weights)
        given = partial(tick, 1, sibling, gains[0], weights)
        part = part + to_sibling(given).astype(jnp.float32)
        slots = [step if chips & (chips - 1) == 0 else (chips - step) % chips for step in range(chips)]
        sums = [part[slot * height : (slot + 1) * height] for slot in slots]
        sums[0] = sums[0] + x.astype(jnp.float32)
        if tick + 1 < ticks:
            sums = lax.optimization_barrier([part.astype(jnp.bfloat16) for part in sums])
            sums = [to_next(part, tick + 1, step) for step, part in enumerate(sums)]
        else:
            sums[1:] = [to_chip(part.astype(jnp.bfloat16), step) for step, part in enumerate(sums) if step > 0]
        state = summed(sums[::-1] if tick + 1 < ticks else sums)
        if tick + 1 < ticks:
            state = jnp.where((section == 0) & (role_at(tick + 1) == 0), entering[tick], state)

    role = role_at(ticks - 1)
    kept = jnp.where(core == 0, state[:rows], state[rows:])
    received = to_sibling(jnp.where(core == 0, state[rows:], state[:rows]))
    down_state = jnp.where(role == 0, kept, received)
    up_state = jnp.where(role == 0, received, kept)
    return (down_state[None], up_state[None])


def solution(mesh):
    return jax.shard_map(
        on_device,
        mesh=mesh,
        in_specs=(
            P("pipe", "zero", None),
            P("pipe", "zero", None),
            P(None, "zero", None),
            P(),
            P("pipe", None, None),
            P("pipe", None, None, "zero"),
            P("pipe", None, None, "zero"),
            P("pipe", None, "zero", None),
        ),
        out_specs=(P("pipe", "zero", None), P("pipe", "zero", None)),
        check_vma=False,
    )
```

```python
import functools

import jax
import jax.numpy as jnp
from jax import lax
from jax.experimental import pallas as pl
from jax.experimental.pallas import tpu as pltpu
from jax.sharding import PartitionSpec as P

CORES = 2
EPS = 1e-05
LIMIT = 8 * 2**20
BESIDE = 10**10


def normalize(x, gain):
    xf = x.astype(jnp.float32)
    return (xf * lax.rsqrt(jnp.mean(xf * xf, axis=-1, keepdims=True) + EPS) * gain).astype(jnp.bfloat16)


def role_at(tick):
    return (lax.axis_index("pipe") + lax.axis_index("zero") % CORES + tick) % 2


def group_kernel(tick, other, ready, mark_ref, gains_ref, gate_ref, up_ref, down_ref, *refs):
    group = (role_at(tick) + other) % 2
    normed = jnp.concatenate([ref[...] for ref in refs[:-1]], axis=0)
    if not ready:
        normed = normalize(normed, gains_ref[pl.ds(group, 1), :])
    gate = jnp.dot(normed, gate_ref[group], preferred_element_type=jnp.float32)
    up = jnp.dot(normed, up_ref[group], preferred_element_type=jnp.float32)
    hidden = (gate / (1.0 + jnp.exp(-gate)) * up).astype(jnp.bfloat16)
    refs[-1][...] = jnp.dot(hidden, down_ref[group], preferred_element_type=jnp.float32).astype(refs[-1].dtype)


def pass_kernel(x_ref, out):
    out[...] = x_ref[...]


def passed(x):
    vmem = pl.BlockSpec(memory_space=pltpu.VMEM)
    return pl.pallas_call(
        pass_kernel,
        out_shape=jax.ShapeDtypeStruct(x.shape, x.dtype),
        in_specs=[vmem],
        out_specs=vmem,
        compiler_params=pltpu.CompilerParams(vmem_limit_bytes=LIMIT),
        cost_estimate=pl.CostEstimate(flops=BESIDE, bytes_accessed=4 * x.size, transcendentals=0),
    )(x)


def sum_kernel(*refs):
    total = refs[0][...].astype(jnp.float32)
    for ref in refs[1:-1]:
        total += ref[...].astype(jnp.float32)
    refs[-1][...] = total.astype(refs[-1].dtype)


def summed(parts):
    vmem = pl.BlockSpec(memory_space=pltpu.VMEM)
    return pl.pallas_call(
        sum_kernel,
        out_shape=jax.ShapeDtypeStruct(parts[0].shape, jnp.bfloat16),
        in_specs=[vmem] * len(parts),
        out_specs=vmem,
        compiler_params=pltpu.CompilerParams(vmem_limit_bytes=LIMIT),
    )(*parts)


def next_kernel(tick, gains_ref, entering_ref, *refs):
    *parts, x_out, normed_out = refs
    total = parts[0][...].astype(jnp.float32)
    for part in parts[1:]:
        total += part[...].astype(jnp.float32)
    role = role_at(tick)
    entry = (lax.axis_index("pipe") == 0) & (role == 0)
    x = jnp.where(entry, entering_ref[...].astype(jnp.float32), total).astype(x_out.dtype)
    x_out[...] = x
    normed_out[...] = normalize(x, gains_ref[pl.ds(role, 1), :])


def next_rows(tick, gains, entering, parts):
    vmem = pl.BlockSpec(memory_space=pltpu.VMEM)
    shape = jax.ShapeDtypeStruct(entering.shape, entering.dtype)
    return pl.pallas_call(
        functools.partial(next_kernel, tick),
        out_shape=(shape, shape),
        in_specs=[vmem] * (2 + len(parts)),
        out_specs=(vmem, vmem),
        compiler_params=pltpu.CompilerParams(vmem_limit_bytes=LIMIT),
    )(gains, entering, *parts)


def partial(tick, other, ready, pieces, gains, weights, mark):
    vmem = pl.BlockSpec(memory_space=pltpu.VMEM)
    rows, width = len(pieces) * mark.shape[0], mark.shape[1]
    size = sum(w.size // w.shape[0] for w in weights)
    return pl.pallas_call(
        functools.partial(group_kernel, tick, other, ready),
        out_shape=jax.ShapeDtypeStruct((rows, width), jnp.bfloat16 if other else jnp.float32),
        in_specs=[vmem] * (2 + len(weights) + len(pieces)),
        out_specs=vmem,
        compiler_params=pltpu.CompilerParams(vmem_limit_bytes=LIMIT),
        cost_estimate=pl.CostEstimate(flops=2 * rows * size, bytes_accessed=2 * size, transcendentals=0),
    )(mark, gains, *weights, *pieces)


def chip_pairs(chips, step):
    if chips & (chips - 1) == 0:
        return [(chip, chip ^ step) for chip in range(chips)]
    return [(chip, (chip + step) % chips) for chip in range(chips)]


def on_device(down_out, up_out, feeds, order, gains, gate_w, up_w, down_w):
    sections, zero = lax.axis_size("pipe"), lax.axis_size("zero")
    chips = zero // CORES
    section, place = lax.axis_index("pipe"), lax.axis_index("zero")
    core = place % CORES
    ticks = feeds.shape[0]
    both = ("pipe", "zero")

    def to_sibling(value):
        return lax.ppermute(value, "zero", [(k, k ^ 1) for k in range(zero)])

    def to_chip(value, step):
        pairs = [(a * CORES + r, b * CORES + r) for a, b in chip_pairs(chips, step) for r in range(CORES)]
        return lax.ppermute(value, "zero", pairs)

    def to_next(value, tick, step):
        pairs = []
        for s in range(sections):
            for r in range(CORES):
                other = s - 1 if (s + r + tick) % 2 == 0 else s + 1
                other = other if 0 <= other < sections else s
                for a, b in chip_pairs(chips, step):
                    pairs.append((s * zero + a * CORES + r, other * zero + b * CORES + r))
        return lax.ppermute(value, both, pairs)

    def joined(own, other):
        first = jnp.where(core == 0, own, other)
        second = jnp.where(core == 0, other, own)
        return jnp.concatenate([first, second], axis=0)

    weights = (gate_w[0], up_w[0], down_w[0])
    place_in_pipe = jnp.full((1, ticks), section, jnp.float32)
    numbers = jnp.arange(ticks) + (passed(place_in_pipe)[0] - place_in_pipe[0]).astype(order.dtype)
    chosen = (order[:, None] == numbers[None, :]).astype(feeds.dtype)
    fed = jnp.einsum("tn,nrd->trd", chosen, feeds, preferred_element_type=jnp.float32).astype(feeds.dtype)
    was_down = role_at(1) == 0
    ascended = jnp.where(section == 0, fed[0], up_out[0])
    given = jnp.where(was_down, ascended, down_out[0])
    own = jnp.where(was_down, down_out[0], ascended)
    rows = own.shape[0]
    given = jnp.concatenate([given] + [fed[tick] for tick in range(1, ticks)], axis=0)
    own, given = lax.optimization_barrier((own, given))
    taken = to_sibling(given)
    state = joined(own, taken[:rows])
    entering = [joined(given[rows * tick : rows * (tick + 1)], taken[rows * tick : rows * (tick + 1)]) for tick in range(1, ticks)]

    for tick in range(ticks):
        if tick == 0:
            pieces = [to_next(state, tick, step) for step in range(chips)]
        else:
            pieces = [normed] + [to_chip(normed, step) for step in range(1, chips)]
        x = pieces[0] if tick == 0 else state
        height = x.shape[0]
        mark = passed(state)
        pieces = pieces[::-1]
        siblings = [to_sibling(piece) for piece in pieces]
        part = partial(tick, 0, tick > 0, pieces, gains[0], weights, mark)
        given = partial(tick, 1, tick > 0, siblings, gains[0], weights, mark)
        part = part + to_sibling(given).astype(jnp.float32)
        slots = [step if chips & (chips - 1) == 0 else (chips - step) % chips for step in range(chips)]
        sums = [part[(chips - 1 - slot) * height : (chips - slot) * height] for slot in slots]
        sums[0] = sums[0] + x.astype(jnp.float32)
        if tick + 1 < ticks:
            sums = lax.optimization_barrier([part.astype(jnp.bfloat16) for part in sums])
            sums = [to_next(part, tick + 1, step) for step, part in enumerate(sums)]
        else:
            sums[1:] = [to_chip(part.astype(jnp.bfloat16), step) for step, part in enumerate(sums) if step > 0]
        if tick + 1 < ticks:
            state, normed = next_rows(tick + 1, gains[0], entering[tick], sums[::-1])
        else:
            state = summed(sums[::-1])

    role = role_at(ticks - 1)
    kept = jnp.where(core == 0, state[:rows], state[rows:])
    received = to_sibling(jnp.where(core == 0, state[rows:], state[:rows]))
    down_state = jnp.where(role == 0, kept, received)
    up_state = jnp.where(role == 0, received, kept)
    return (down_state[None], up_state[None])


def solution(mesh):
    return jax.shard_map(
        on_device,
        mesh=mesh,
        in_specs=(
            P("pipe", "zero", None),
            P("pipe", "zero", None),
            P(None, "zero", None),
            P(),
            P("pipe", None, None),
            P("pipe", None, None, "zero"),
            P("pipe", None, None, "zero"),
            P("pipe", None, "zero", None),
        ),
        out_specs=(P("pipe", "zero", None), P("pipe", "zero", None)),
        check_vma=False,
    )
```

```python
import functools

import jax
import jax.numpy as jnp
from jax import lax
from jax.experimental import pallas as pl
from jax.experimental.pallas import tpu as pltpu
from jax.sharding import PartitionSpec as P

CORES = 2
EPS = 1e-05
LIMIT = 8 * 2**20
BESIDE = 10**10


def normalize(x, gain):
    xf = x.astype(jnp.float32)
    return (xf * lax.rsqrt(jnp.mean(xf * xf, axis=-1, keepdims=True) + EPS) * gain).astype(jnp.bfloat16)


def role_at(tick):
    return (lax.axis_index("pipe") + lax.axis_index("zero") % CORES + tick) % 2


def group_kernel(tick, other, ready, count, chips, mark_ref, gains_ref, gate_ref, up_ref, down_ref, *refs):
    group = (role_at(tick) + other) % 2
    pieces, outs = refs[:count], refs[count:]
    normed = jnp.concatenate([ref[...] for ref in pieces], axis=0)
    if not ready:
        normed = normalize(normed, gains_ref[pl.ds(group, 1), :])
    gate = jnp.dot(normed, gate_ref[group], preferred_element_type=jnp.float32)
    up = jnp.dot(normed, up_ref[group], preferred_element_type=jnp.float32)
    hidden = (gate / (1.0 + jnp.exp(-gate)) * up).astype(jnp.bfloat16)
    part = jnp.dot(hidden, down_ref[group], preferred_element_type=jnp.float32)
    if len(outs) == 1:
        outs[0][...] = part.astype(outs[0].dtype)
        return
    first_core = lax.axis_index("zero") % CORES == 0
    rows = part.shape[0] // (CORES * chips)
    halves = [part[n * rows : (n + 1) * rows] for n in range(CORES * chips)]
    keep = [jnp.where(first_core, a, b) for a, b in zip(halves[::2], halves[1::2])]
    give = [jnp.where(first_core, b, a) for a, b in zip(halves[::2], halves[1::2])]
    outs[0][...] = jnp.concatenate(keep, axis=0).astype(outs[0].dtype)
    outs[1][...] = jnp.concatenate(give, axis=0).astype(outs[1].dtype)


def pass_kernel(x_ref, out):
    out[...] = x_ref[...]


def passed(x):
    vmem = pl.BlockSpec(memory_space=pltpu.VMEM)
    return pl.pallas_call(
        pass_kernel,
        out_shape=jax.ShapeDtypeStruct(x.shape, x.dtype),
        in_specs=[vmem],
        out_specs=vmem,
        compiler_params=pltpu.CompilerParams(vmem_limit_bytes=LIMIT),
        cost_estimate=pl.CostEstimate(flops=BESIDE, bytes_accessed=4 * x.size, transcendentals=0),
    )(x)


def stack_kernel(mark_ref, *refs):
    height = refs[0].shape[0]
    for slot, ref in enumerate(refs[:-1]):
        refs[-1][slot * height : (slot + 1) * height] = ref[...]


def stacked(pieces, mark):
    vmem = pl.BlockSpec(memory_space=pltpu.VMEM)
    rows, width = mark.shape
    return pl.pallas_call(
        stack_kernel,
        out_shape=jax.ShapeDtypeStruct((len(pieces) * rows, width), mark.dtype),
        in_specs=[vmem] * (1 + len(pieces)),
        out_specs=vmem,
        compiler_params=pltpu.CompilerParams(vmem_limit_bytes=LIMIT),
    )(mark, *pieces)


def sum_kernel(*refs):
    total = refs[0][...].astype(jnp.float32)
    for ref in refs[1:-1]:
        total += ref[...].astype(jnp.float32)
    refs[-1][...] = total.astype(refs[-1].dtype)


def summed(parts):
    vmem = pl.BlockSpec(memory_space=pltpu.VMEM)
    return pl.pallas_call(
        sum_kernel,
        out_shape=jax.ShapeDtypeStruct(parts[0].shape, jnp.bfloat16),
        in_specs=[vmem] * len(parts),
        out_specs=vmem,
        compiler_params=pltpu.CompilerParams(vmem_limit_bytes=LIMIT),
    )(*parts)


def next_kernel(tick, gains_ref, entering_ref, *refs):
    *parts, x_out, normed_out = refs
    total = parts[0][...].astype(jnp.float32)
    for part in parts[1:]:
        total += part[...].astype(jnp.float32)
    role = role_at(tick)
    entry = (lax.axis_index("pipe") == 0) & (role == 0)
    x = jnp.where(entry, entering_ref[...].astype(jnp.float32), total).astype(x_out.dtype)
    x_out[...] = x
    normed_out[...] = normalize(x, gains_ref[pl.ds(role, 1), :])


def next_rows(tick, gains, entering, parts):
    vmem = pl.BlockSpec(memory_space=pltpu.VMEM)
    shape = jax.ShapeDtypeStruct(entering.shape, entering.dtype)
    return pl.pallas_call(
        functools.partial(next_kernel, tick),
        out_shape=(shape, shape),
        in_specs=[vmem] * (2 + len(parts)),
        out_specs=(vmem, vmem),
        compiler_params=pltpu.CompilerParams(vmem_limit_bytes=LIMIT),
    )(gains, entering, *parts)


def partial(tick, other, ready, split, chips, pieces, gains, weights, mark):
    vmem = pl.BlockSpec(memory_space=pltpu.VMEM)
    rows, width = chips * mark.shape[0], mark.shape[1]
    size = sum(w.size // w.shape[0] for w in weights)
    out = jax.ShapeDtypeStruct((rows, width), jnp.bfloat16 if other else jnp.float32)
    if split:
        out = tuple(jax.ShapeDtypeStruct((rows // CORES, width), dtype) for dtype in (jnp.float32, jnp.bfloat16))
    return pl.pallas_call(
        functools.partial(group_kernel, tick, other, ready, len(pieces), chips),
        out_shape=out,
        in_specs=[vmem] * (2 + len(weights) + len(pieces)),
        out_specs=(vmem, vmem) if split else vmem,
        compiler_params=pltpu.CompilerParams(vmem_limit_bytes=LIMIT),
        cost_estimate=pl.CostEstimate(flops=2 * rows * size, bytes_accessed=2 * size, transcendentals=0),
    )(mark, gains, *weights, *pieces)


def chip_pairs(chips, step):
    if chips & (chips - 1) == 0:
        return [(chip, chip ^ step) for chip in range(chips)]
    return [(chip, (chip + step) % chips) for chip in range(chips)]


def on_device(down_out, up_out, feeds, order, gains, gate_w, up_w, down_w):
    sections, zero = lax.axis_size("pipe"), lax.axis_size("zero")
    chips = zero // CORES
    section, place = lax.axis_index("pipe"), lax.axis_index("zero")
    core = place % CORES
    ticks = feeds.shape[0]
    both = ("pipe", "zero")

    def to_sibling(value):
        return lax.ppermute(value, "zero", [(k, k ^ 1) for k in range(zero)])

    def to_chip(value, step):
        pairs = [(a * CORES + r, b * CORES + r) for a, b in chip_pairs(chips, step) for r in range(CORES)]
        return lax.ppermute(value, "zero", pairs)

    def to_next(value, tick, step):
        pairs = []
        for s in range(sections):
            for r in range(CORES):
                other = s - 1 if (s + r + tick) % 2 == 0 else s + 1
                other = other if 0 <= other < sections else s
                for a, b in chip_pairs(chips, step):
                    pairs.append((s * zero + a * CORES + r, other * zero + b * CORES + r))
        return lax.ppermute(value, both, pairs)

    def joined(own, other):
        first = jnp.where(core == 0, own, other)
        second = jnp.where(core == 0, other, own)
        return jnp.concatenate([first, second], axis=0)

    weights = (gate_w[0], up_w[0], down_w[0])
    place_in_pipe = jnp.full((1, ticks), section, jnp.float32)
    numbers = jnp.arange(ticks) + (passed(place_in_pipe)[0] - place_in_pipe[0]).astype(order.dtype)
    chosen = (order[:, None] == numbers[None, :]).astype(feeds.dtype)
    fed = jnp.einsum("tn,nrd->trd", chosen, feeds, preferred_element_type=jnp.float32).astype(feeds.dtype)
    was_down = role_at(1) == 0
    ascended = jnp.where(section == 0, fed[0], up_out[0])
    given = jnp.where(was_down, ascended, down_out[0])
    own = jnp.where(was_down, down_out[0], ascended)
    rows = own.shape[0]
    given = jnp.concatenate([given] + [fed[tick] for tick in range(1, ticks)], axis=0)
    own, given = lax.optimization_barrier((own, given))
    taken = to_sibling(given)
    state = joined(own, taken[:rows])
    entering = [joined(given[rows * tick : rows * (tick + 1)], taken[rows * tick : rows * (tick + 1)]) for tick in range(1, ticks)]

    for tick in range(ticks):
        if tick == 0:
            pieces = [to_next(state, tick, step) for step in range(chips)]
        else:
            pieces = [normed] + [to_chip(normed, step) for step in range(1, chips)]
        x = pieces[0] if tick == 0 else state
        height = x.shape[0]
        mark = passed(state)
        slots = [step if chips & (chips - 1) == 0 else (chips - step) % chips for step in range(chips)]
        if tick + 1 == ticks:
            break
        siblings = [to_sibling(piece) for piece in pieces]
        part = partial(tick, 0, tick > 0, False, chips, pieces, gains[0], weights, mark)
        given = partial(tick, 1, tick > 0, False, chips, siblings, gains[0], weights, mark)
        part = part + to_sibling(given).astype(jnp.float32)
        sums = [part[slot * height : (slot + 1) * height] for slot in slots]
        sums[0] = sums[0] + x.astype(jnp.float32)
        sums = lax.optimization_barrier([part.astype(jnp.bfloat16) for part in sums])
        sums = [to_next(part, tick + 1, step) for step, part in enumerate(sums)]
        state, normed = next_rows(tick + 1, gains[0], entering[tick], sums[::-1])

    rows_here = jnp.where(core == 0, x[:rows], x[rows:])
    rows_there = to_sibling(jnp.where(core == 0, x[rows:], x[:rows]))
    stack = stacked(pieces, mark)
    mine, given = partial(tick, 0, tick > 0, True, chips, [stack], gains[0], weights, mark)
    theirs, back = partial(tick, 1, tick > 0, True, chips, [to_sibling(stack)], gains[0], weights, mark)
    theirs = theirs + to_sibling(given).astype(jnp.float32)
    mine = mine + to_sibling(back).astype(jnp.float32)
    sums = [
        jnp.concatenate([part[slot * rows : (slot + 1) * rows] for part in (mine, theirs)], axis=0) for slot in slots
    ]
    sums[0] = sums[0] + jnp.concatenate([rows_here, rows_there], axis=0).astype(jnp.float32)
    sums[1:] = lax.optimization_barrier([part.astype(jnp.bfloat16) for part in sums[1:]])
    sums[1:] = [to_chip(part, step) for step, part in enumerate(sums) if step > 0]
    state = summed(sums[::-1])
    role = role_at(ticks - 1)
    down_state = jnp.where(role == 0, state[:rows], state[rows:])
    up_state = jnp.where(role == 0, state[rows:], state[:rows])
    return (down_state[None], up_state[None])


def solution(mesh):
    return jax.shard_map(
        on_device,
        mesh=mesh,
        in_specs=(
            P("pipe", "zero", None),
            P("pipe", "zero", None),
            P(None, "zero", None),
            P(),
            P("pipe", None, None),
            P("pipe", None, None, "zero"),
            P("pipe", None, None, "zero"),
            P("pipe", None, "zero", None),
        ),
        out_specs=(P("pipe", "zero", None), P("pipe", "zero", None)),
        check_vma=False,
    )
```

```python
import functools

import jax
import jax.numpy as jnp
from jax import lax
from jax.experimental import pallas as pl
from jax.experimental.pallas import tpu as pltpu
from jax.sharding import PartitionSpec as P

CORES = 2
EPS = 1e-05
BLOCK = 128
LIMIT = 8 * 2**20
BESIDE = 10**10


def normalize(x, gain):
    xf = x.astype(jnp.float32)
    return (xf * lax.rsqrt(jnp.mean(xf * xf, axis=-1, keepdims=True) + EPS) * gain).astype(jnp.bfloat16)


def role_at(tick):
    return (lax.axis_index("pipe") + lax.axis_index("zero") % CORES + tick) % 2


def group_kernel(tick, other, ready, count, chips, mark_ref, gains_ref, gate_ref, up_ref, down_ref, *refs):
    group = (role_at(tick) + other) % 2
    pieces, outs = refs[:count], refs[count:]
    normed = jnp.concatenate([ref[...] for ref in pieces], axis=0)
    if not ready:
        normed = normalize(normed, gains_ref[pl.ds(group, 1), :])
    hidden = []
    for first in range(0, gate_ref.shape[2], BLOCK):
        block = pl.ds(first, BLOCK)
        gate = jnp.dot(normed, gate_ref[group, :, block], preferred_element_type=jnp.float32)
        up = jnp.dot(normed, up_ref[group, :, block], preferred_element_type=jnp.float32)
        hidden.append((gate / (1.0 + jnp.exp(-gate)) * up).astype(jnp.bfloat16))
    hidden = jnp.concatenate(hidden, axis=1)
    first_core = lax.axis_index("zero") % CORES == 0
    for first in range(0, down_ref.shape[2], BLOCK):
        block = pl.ds(first, BLOCK)
        part = jnp.dot(hidden, down_ref[group, :, block], preferred_element_type=jnp.float32)
        if len(outs) == 1:
            outs[0][:, block] = part.astype(outs[0].dtype)
            continue
        rows = part.shape[0] // (CORES * chips)
        halves = [part[n * rows : (n + 1) * rows] for n in range(CORES * chips)]
        keep = [jnp.where(first_core, a, b) for a, b in zip(halves[::2], halves[1::2])]
        give = [jnp.where(first_core, b, a) for a, b in zip(halves[::2], halves[1::2])]
        outs[0][:, block] = jnp.concatenate(keep, axis=0).astype(outs[0].dtype)
        outs[1][:, block] = jnp.concatenate(give, axis=0).astype(outs[1].dtype)


def pass_kernel(x_ref, out):
    out[...] = x_ref[...]


def passed(x):
    vmem = pl.BlockSpec(memory_space=pltpu.VMEM)
    return pl.pallas_call(
        pass_kernel,
        out_shape=jax.ShapeDtypeStruct(x.shape, x.dtype),
        in_specs=[vmem],
        out_specs=vmem,
        compiler_params=pltpu.CompilerParams(vmem_limit_bytes=LIMIT),
        cost_estimate=pl.CostEstimate(flops=BESIDE, bytes_accessed=4 * x.size, transcendentals=0),
    )(x)


def stack_kernel(mark_ref, *refs):
    height = refs[0].shape[0]
    for slot, ref in enumerate(refs[:-1]):
        refs[-1][slot * height : (slot + 1) * height] = ref[...]


def stacked(pieces, mark):
    vmem = pl.BlockSpec(memory_space=pltpu.VMEM)
    rows, width = mark.shape
    return pl.pallas_call(
        stack_kernel,
        out_shape=jax.ShapeDtypeStruct((len(pieces) * rows, width), mark.dtype),
        in_specs=[vmem] * (1 + len(pieces)),
        out_specs=vmem,
        compiler_params=pltpu.CompilerParams(vmem_limit_bytes=LIMIT),
    )(mark, *pieces)


def sum_kernel(*refs):
    total = refs[0][...].astype(jnp.float32)
    for ref in refs[1:-1]:
        total += ref[...].astype(jnp.float32)
    refs[-1][...] = total.astype(refs[-1].dtype)


def summed(parts):
    vmem = pl.BlockSpec(memory_space=pltpu.VMEM)
    return pl.pallas_call(
        sum_kernel,
        out_shape=jax.ShapeDtypeStruct(parts[0].shape, jnp.bfloat16),
        in_specs=[vmem] * len(parts),
        out_specs=vmem,
        compiler_params=pltpu.CompilerParams(vmem_limit_bytes=LIMIT),
    )(*parts)


def next_kernel(tick, gains_ref, entering_ref, *refs):
    *parts, x_out, normed_out = refs
    total = parts[0][...].astype(jnp.float32)
    for part in parts[1:]:
        total += part[...].astype(jnp.float32)
    role = role_at(tick)
    entry = (lax.axis_index("pipe") == 0) & (role == 0)
    x = jnp.where(entry, entering_ref[...].astype(jnp.float32), total).astype(x_out.dtype)
    x_out[...] = x
    normed_out[...] = normalize(x, gains_ref[pl.ds(role, 1), :])


def next_rows(tick, gains, entering, parts):
    vmem = pl.BlockSpec(memory_space=pltpu.VMEM)
    shape = jax.ShapeDtypeStruct(entering.shape, entering.dtype)
    return pl.pallas_call(
        functools.partial(next_kernel, tick),
        out_shape=(shape, shape),
        in_specs=[vmem] * (2 + len(parts)),
        out_specs=(vmem, vmem),
        compiler_params=pltpu.CompilerParams(vmem_limit_bytes=LIMIT),
    )(gains, entering, *parts)


def partial(tick, other, ready, split, chips, pieces, gains, weights, mark):
    vmem = pl.BlockSpec(memory_space=pltpu.VMEM)
    rows, width = chips * mark.shape[0], mark.shape[1]
    size = sum(w.size // w.shape[0] for w in weights)
    out = jax.ShapeDtypeStruct((rows, width), jnp.bfloat16 if other else jnp.float32)
    if split:
        out = tuple(jax.ShapeDtypeStruct((rows // CORES, width), dtype) for dtype in (jnp.float32, jnp.bfloat16))
    return pl.pallas_call(
        functools.partial(group_kernel, tick, other, ready, len(pieces), chips),
        out_shape=out,
        in_specs=[vmem] * (2 + len(weights) + len(pieces)),
        out_specs=(vmem, vmem) if split else vmem,
        compiler_params=pltpu.CompilerParams(vmem_limit_bytes=LIMIT),
        cost_estimate=pl.CostEstimate(flops=2 * rows * size, bytes_accessed=2 * size, transcendentals=0),
    )(mark, gains, *weights, *pieces)


def chip_pairs(chips, step):
    if chips & (chips - 1) == 0:
        return [(chip, chip ^ step) for chip in range(chips)]
    return [(chip, (chip + step) % chips) for chip in range(chips)]


def on_device(down_out, up_out, feeds, order, gains, gate_w, up_w, down_w):
    sections, zero = lax.axis_size("pipe"), lax.axis_size("zero")
    chips = zero // CORES
    section, place = lax.axis_index("pipe"), lax.axis_index("zero")
    core = place % CORES
    ticks = feeds.shape[0]
    both = ("pipe", "zero")

    def to_sibling(value):
        return lax.ppermute(value, "zero", [(k, k ^ 1) for k in range(zero)])

    def to_chip(value, step):
        pairs = [(a * CORES + r, b * CORES + r) for a, b in chip_pairs(chips, step) for r in range(CORES)]
        return lax.ppermute(value, "zero", pairs)

    def to_next(value, tick, step):
        pairs = []
        for s in range(sections):
            for r in range(CORES):
                other = s - 1 if (s + r + tick) % 2 == 0 else s + 1
                other = other if 0 <= other < sections else s
                for a, b in chip_pairs(chips, step):
                    pairs.append((s * zero + a * CORES + r, other * zero + b * CORES + r))
        return lax.ppermute(value, both, pairs)

    def joined(own, other):
        first = jnp.where(core == 0, own, other)
        second = jnp.where(core == 0, other, own)
        return jnp.concatenate([first, second], axis=0)

    weights = (gate_w[0], up_w[0], down_w[0])
    place_in_pipe = jnp.full((1, ticks), section, jnp.float32)
    numbers = jnp.arange(ticks) + (passed(place_in_pipe)[0] - place_in_pipe[0]).astype(order.dtype)
    chosen = (order[:, None] == numbers[None, :]).astype(feeds.dtype)
    fed = jnp.einsum("tn,nrd->trd", chosen, feeds, preferred_element_type=jnp.float32).astype(feeds.dtype)
    was_down = role_at(1) == 0
    ascended = jnp.where(section == 0, fed[0], up_out[0])
    given = jnp.where(was_down, ascended, down_out[0])
    own = jnp.where(was_down, down_out[0], ascended)
    rows = own.shape[0]
    given = jnp.concatenate([given] + [fed[tick] for tick in range(1, ticks)], axis=0)
    own, given = lax.optimization_barrier((own, given))
    taken = to_sibling(given)
    state = joined(own, taken[:rows])
    entering = [joined(given[rows * tick : rows * (tick + 1)], taken[rows * tick : rows * (tick + 1)]) for tick in range(1, ticks)]

    for tick in range(ticks):
        if tick == 0:
            pieces = [to_next(state, tick, step) for step in range(chips)]
        else:
            pieces = [normed] + [to_chip(normed, step) for step in range(1, chips)]
        x = pieces[0] if tick == 0 else state
        height = x.shape[0]
        mark = passed(state)
        slots = [step if chips & (chips - 1) == 0 else (chips - step) % chips for step in range(chips)]
        if tick + 1 == ticks:
            break
        siblings = [to_sibling(piece) for piece in pieces]
        part = partial(tick, 0, tick > 0, False, chips, pieces, gains[0], weights, mark)
        given = partial(tick, 1, tick > 0, False, chips, siblings, gains[0], weights, mark)
        part = part + to_sibling(given).astype(jnp.float32)
        sums = [part[slot * height : (slot + 1) * height] for slot in slots]
        sums[0] = sums[0] + x.astype(jnp.float32)
        sums = lax.optimization_barrier([part.astype(jnp.bfloat16) for part in sums])
        sums = [to_next(part, tick + 1, step) for step, part in enumerate(sums)]
        state, normed = next_rows(tick + 1, gains[0], entering[tick], sums[::-1])

    rows_here = jnp.where(core == 0, x[:rows], x[rows:])
    rows_there = to_sibling(jnp.where(core == 0, x[rows:], x[:rows]))
    stack = stacked(pieces, mark)
    mine, given = partial(tick, 0, tick > 0, True, chips, [stack], gains[0], weights, mark)
    theirs, back = partial(tick, 1, tick > 0, True, chips, [to_sibling(stack)], gains[0], weights, mark)
    theirs = theirs + to_sibling(given).astype(jnp.float32)
    mine = mine + to_sibling(back).astype(jnp.float32)
    sums = [
        jnp.concatenate([part[slot * rows : (slot + 1) * rows] for part in (mine, theirs)], axis=0) for slot in slots
    ]
    sums[0] = sums[0] + jnp.concatenate([rows_here, rows_there], axis=0).astype(jnp.float32)
    sums[1:] = lax.optimization_barrier([part.astype(jnp.bfloat16) for part in sums[1:]])
    sums[1:] = [to_chip(part, step) for step, part in enumerate(sums) if step > 0]
    state = summed(sums[::-1])
    role = role_at(ticks - 1)
    down_state = jnp.where(role == 0, state[:rows], state[rows:])
    up_state = jnp.where(role == 0, state[rows:], state[:rows])
    return (down_state[None], up_state[None])


def solution(mesh):
    return jax.shard_map(
        on_device,
        mesh=mesh,
        in_specs=(
            P("pipe", "zero", None),
            P("pipe", "zero", None),
            P(None, "zero", None),
            P(),
            P("pipe", None, None),
            P("pipe", None, None, "zero"),
            P("pipe", None, None, "zero"),
            P("pipe", None, "zero", None),
        ),
        out_specs=(P("pipe", "zero", None), P("pipe", "zero", None)),
        check_vma=False,
    )
```

```python
import functools

import jax
import jax.numpy as jnp
from jax import lax
from jax.experimental import pallas as pl
from jax.experimental.pallas import tpu as pltpu
from jax.sharding import PartitionSpec as P

CORES = 2
EPS = 1e-05
BLOCK = 128
LIMIT = 8 * 2**20
BESIDE = 10**10


def normalize(x, gain):
    xf = x.astype(jnp.float32)
    return (xf * lax.rsqrt(jnp.mean(xf * xf, axis=-1, keepdims=True) + EPS) * gain).astype(jnp.bfloat16)


def role_at(tick):
    return (lax.axis_index("pipe") + lax.axis_index("zero") % CORES + tick) % 2


def group_kernel(tick, other, ready, count, chips, mark_ref, gains_ref, gate_ref, up_ref, down_ref, *refs):
    group = (role_at(tick) + other) % 2
    pieces, outs = refs[:count], refs[count:]
    normed = jnp.concatenate([ref[...] for ref in pieces], axis=0)
    if not ready:
        normed = normalize(normed, gains_ref[pl.ds(group, 1), :])
    hidden = []
    for first in range(0, gate_ref.shape[2], BLOCK):
        block = pl.ds(first, BLOCK)
        gate = jnp.dot(normed, gate_ref[group, :, block], preferred_element_type=jnp.float32)
        up = jnp.dot(normed, up_ref[group, :, block], preferred_element_type=jnp.float32)
        hidden.append((gate / (1.0 + jnp.exp(-gate)) * up).astype(jnp.bfloat16))
    hidden = jnp.concatenate(hidden, axis=1)
    first_core = lax.axis_index("zero") % CORES == 0
    for first in range(0, down_ref.shape[2], BLOCK):
        block = pl.ds(first, BLOCK)
        part = jnp.dot(hidden, down_ref[group, :, block], preferred_element_type=jnp.float32)
        if len(outs) == 1:
            outs[0][:, block] = part.astype(outs[0].dtype)
            continue
        rows = part.shape[0] // (CORES * chips)
        halves = [part[n * rows : (n + 1) * rows] for n in range(CORES * chips)]
        keep = [jnp.where(first_core, a, b) for a, b in zip(halves[::2], halves[1::2])]
        give = [jnp.where(first_core, b, a) for a, b in zip(halves[::2], halves[1::2])]
        outs[0][:, block] = jnp.concatenate(keep, axis=0).astype(outs[0].dtype)
        outs[1][:, block] = jnp.concatenate(give, axis=0).astype(outs[1].dtype)


def pass_kernel(x_ref, out):
    out[...] = x_ref[...]


def passed(x):
    vmem = pl.BlockSpec(memory_space=pltpu.VMEM)
    return pl.pallas_call(
        pass_kernel,
        out_shape=jax.ShapeDtypeStruct(x.shape, x.dtype),
        in_specs=[vmem],
        out_specs=vmem,
        compiler_params=pltpu.CompilerParams(vmem_limit_bytes=LIMIT),
        cost_estimate=pl.CostEstimate(flops=BESIDE, bytes_accessed=4 * x.size, transcendentals=0),
    )(x)


def stack_kernel(mark_ref, *refs):
    height = refs[0].shape[0]
    for slot, ref in enumerate(refs[:-1]):
        refs[-1][slot * height : (slot + 1) * height] = ref[...]


def stacked(pieces, mark):
    vmem = pl.BlockSpec(memory_space=pltpu.VMEM)
    rows, width = pieces[0].shape
    return pl.pallas_call(
        stack_kernel,
        out_shape=jax.ShapeDtypeStruct((len(pieces) * rows, width), pieces[0].dtype),
        in_specs=[vmem] * (1 + len(pieces)),
        out_specs=vmem,
        compiler_params=pltpu.CompilerParams(vmem_limit_bytes=LIMIT),
    )(mark, *pieces)


def spread_kernel(slots, part_ref, got_ref, x_ref, *outs):
    height = x_ref.shape[0]
    for step, (slot, out) in enumerate(zip(slots, outs)):
        place = slice(slot * height, (slot + 1) * height)
        total = part_ref[place] + got_ref[place].astype(jnp.float32)
        if step == 0:
            total += x_ref[...].astype(jnp.float32)
        out[...] = total.astype(out.dtype)


def spread(slots, part, got, x):
    vmem = pl.BlockSpec(memory_space=pltpu.VMEM)
    return pl.pallas_call(
        functools.partial(spread_kernel, slots),
        out_shape=(jax.ShapeDtypeStruct(x.shape, x.dtype),) * len(slots),
        in_specs=[vmem] * 3,
        out_specs=(vmem,) * len(slots),
        compiler_params=pltpu.CompilerParams(vmem_limit_bytes=LIMIT),
    )(part, got, x)


def spread_rows_kernel(slots, mine_ref, theirs_ref, to_mine_ref, to_theirs_ref, here_ref, there_ref, *outs):
    rows = here_ref.shape[0]
    groups = (mine_ref, to_mine_ref, here_ref), (theirs_ref, to_theirs_ref, there_ref)
    for step, (slot, out) in enumerate(zip(slots, outs)):
        place = slice(slot * rows, (slot + 1) * rows)
        totals = [part[place] + got[place].astype(jnp.float32) for part, got, x in groups]
        if step == 0:
            totals = [total + x[...].astype(jnp.float32) for total, (part, got, x) in zip(totals, groups)]
        out[...] = jnp.concatenate(totals, axis=0).astype(out.dtype)


def spread_rows(slots, mine, theirs, to_mine, to_theirs, here, there):
    vmem = pl.BlockSpec(memory_space=pltpu.VMEM)
    rows, width = here.shape
    return pl.pallas_call(
        functools.partial(spread_rows_kernel, slots),
        out_shape=tuple(
            jax.ShapeDtypeStruct((2 * rows, width), jnp.float32 if step == 0 else here.dtype)
            for step in range(len(slots))
        ),
        in_specs=[vmem] * 6,
        out_specs=(vmem,) * len(slots),
        compiler_params=pltpu.CompilerParams(vmem_limit_bytes=LIMIT),
    )(mine, theirs, to_mine, to_theirs, here, there)


def sum_kernel(*refs):
    total = refs[0][...].astype(jnp.float32)
    for ref in refs[1:-1]:
        total += ref[...].astype(jnp.float32)
    refs[-1][...] = total.astype(refs[-1].dtype)


def summed(parts):
    vmem = pl.BlockSpec(memory_space=pltpu.VMEM)
    return pl.pallas_call(
        sum_kernel,
        out_shape=jax.ShapeDtypeStruct(parts[0].shape, jnp.bfloat16),
        in_specs=[vmem] * len(parts),
        out_specs=vmem,
        compiler_params=pltpu.CompilerParams(vmem_limit_bytes=LIMIT),
    )(*parts)


def next_kernel(tick, gains_ref, entering_ref, *refs):
    *parts, x_out, normed_out = refs
    total = parts[0][...].astype(jnp.float32)
    for part in parts[1:]:
        total += part[...].astype(jnp.float32)
    role = role_at(tick)
    entry = (lax.axis_index("pipe") == 0) & (role == 0)
    x = jnp.where(entry, entering_ref[...].astype(jnp.float32), total).astype(x_out.dtype)
    x_out[...] = x
    normed_out[...] = normalize(x, gains_ref[pl.ds(role, 1), :])


def next_rows(tick, gains, entering, parts):
    vmem = pl.BlockSpec(memory_space=pltpu.VMEM)
    shape = jax.ShapeDtypeStruct(entering.shape, entering.dtype)
    return pl.pallas_call(
        functools.partial(next_kernel, tick),
        out_shape=(shape, shape),
        in_specs=[vmem] * (2 + len(parts)),
        out_specs=(vmem, vmem),
        compiler_params=pltpu.CompilerParams(vmem_limit_bytes=LIMIT),
    )(gains, entering, *parts)


def partial(tick, other, ready, split, chips, pieces, gains, weights, mark):
    vmem = pl.BlockSpec(memory_space=pltpu.VMEM)
    rows, width = sum(piece.shape[0] for piece in pieces), pieces[0].shape[1]
    size = sum(w.size // w.shape[0] for w in weights)
    out = jax.ShapeDtypeStruct((rows, width), jnp.bfloat16 if other else jnp.float32)
    if split:
        out = tuple(jax.ShapeDtypeStruct((rows // CORES, width), dtype) for dtype in (jnp.float32, jnp.bfloat16))
    return pl.pallas_call(
        functools.partial(group_kernel, tick, other, ready, len(pieces), chips),
        out_shape=out,
        in_specs=[vmem] * (2 + len(weights) + len(pieces)),
        out_specs=(vmem, vmem) if split else vmem,
        compiler_params=pltpu.CompilerParams(vmem_limit_bytes=LIMIT),
        cost_estimate=pl.CostEstimate(flops=2 * rows * size, bytes_accessed=2 * size, transcendentals=0),
    )(mark, gains, *weights, *pieces)


def chip_pairs(chips, step):
    if chips & (chips - 1) == 0:
        return [(chip, chip ^ step) for chip in range(chips)]
    return [(chip, (chip + step) % chips) for chip in range(chips)]


def on_device(down_out, up_out, feeds, order, gains, gate_w, up_w, down_w):
    sections, zero = lax.axis_size("pipe"), lax.axis_size("zero")
    chips = zero // CORES
    section, place = lax.axis_index("pipe"), lax.axis_index("zero")
    core = place % CORES
    ticks = feeds.shape[0]
    both = ("pipe", "zero")

    def to_sibling(value):
        return lax.ppermute(value, "zero", [(k, k ^ 1) for k in range(zero)])

    def to_chip(value, step):
        pairs = [(a * CORES + r, b * CORES + r) for a, b in chip_pairs(chips, step) for r in range(CORES)]
        return lax.ppermute(value, "zero", pairs)

    def to_next(value, tick, step):
        pairs = []
        for s in range(sections):
            for r in range(CORES):
                other = s - 1 if (s + r + tick) % 2 == 0 else s + 1
                other = other if 0 <= other < sections else s
                for a, b in chip_pairs(chips, step):
                    pairs.append((s * zero + a * CORES + r, other * zero + b * CORES + r))
        return lax.ppermute(value, both, pairs)

    def joined(own, other):
        first = jnp.where(core == 0, own, other)
        second = jnp.where(core == 0, other, own)
        return jnp.concatenate([first, second], axis=0)

    weights = (gate_w[0], up_w[0], down_w[0])
    place_in_pipe = jnp.full((1, ticks), section, jnp.float32)
    numbers = jnp.arange(ticks) + (passed(place_in_pipe)[0] - place_in_pipe[0]).astype(order.dtype)
    chosen = (order[:, None] == numbers[None, :]).astype(feeds.dtype)
    fed = jnp.einsum("tn,nrd->trd", chosen, feeds, preferred_element_type=jnp.float32).astype(feeds.dtype)
    was_down = role_at(1) == 0
    ascended = jnp.where(section == 0, fed[0], up_out[0])
    given = jnp.where(was_down, ascended, down_out[0])
    own = jnp.where(was_down, down_out[0], ascended)
    rows = own.shape[0]
    given = jnp.concatenate([given] + [fed[tick] for tick in range(1, ticks)], axis=0)
    own, given = lax.optimization_barrier((own, given))
    taken = to_sibling(given)
    state = joined(own, taken[:rows])
    entering = [joined(given[rows * tick : rows * (tick + 1)], taken[rows * tick : rows * (tick + 1)]) for tick in range(1, ticks)]

    for tick in range(ticks):
        if tick == 0:
            pieces = [to_next(state, tick, step) for step in range(chips)]
        else:
            pieces = [normed] + [to_chip(normed, step) for step in range(1, chips)]
        x = pieces[0] if tick == 0 else state
        height = x.shape[0]
        mark = passed(state)
        pieces = pieces[::-1]
        slots = [step if chips & (chips - 1) == 0 else (chips - step) % chips for step in range(chips)]
        slots = [chips - 1 - slot for slot in slots]
        if tick + 1 == ticks:
            break
        siblings = [to_sibling(piece) for piece in pieces]
        part = partial(tick, 0, tick > 0, False, chips, pieces, gains[0], weights, mark)
        given = partial(tick, 1, tick > 0, False, chips, siblings, gains[0], weights, mark)
        sums = spread(slots, part, to_sibling(given), x)
        sums = [to_next(part, tick + 1, step) for step, part in enumerate(sums)]
        state, normed = next_rows(tick + 1, gains[0], entering[tick], sums[::-1])

    rows_here = jnp.where(core == 0, x[:rows], x[rows:])
    rows_there = to_sibling(jnp.where(core == 0, x[rows:], x[:rows]))
    stack = stacked(pieces, rows_there)
    mine, given = partial(tick, 0, tick > 0, True, chips, [stack], gains[0], weights, mark)
    theirs, back = partial(tick, 1, tick > 0, True, chips, [to_sibling(stack)], gains[0], weights, mark)
    sums = list(spread_rows(slots, mine, theirs, to_sibling(back), to_sibling(given), rows_here, rows_there))
    sums[1:] = [to_chip(part, step) for step, part in enumerate(sums) if step > 0]
    state = summed(sums[::-1])
    role = role_at(ticks - 1)
    down_state = jnp.where(role == 0, state[:rows], state[rows:])
    up_state = jnp.where(role == 0, state[rows:], state[:rows])
    return (down_state[None], up_state[None])


def solution(mesh):
    return jax.shard_map(
        on_device,
        mesh=mesh,
        in_specs=(
            P("pipe", "zero", None),
            P("pipe", "zero", None),
            P(None, "zero", None),
            P(),
            P("pipe", None, None),
            P("pipe", None, None, "zero"),
            P("pipe", None, None, "zero"),
            P("pipe", None, "zero", None),
        ),
        out_specs=(P("pipe", "zero", None), P("pipe", "zero", None)),
        check_vma=False,
    )
```

```python
import functools

import jax
import jax.numpy as jnp
from jax import lax
from jax.experimental import pallas as pl
from jax.experimental.pallas import tpu as pltpu
from jax.sharding import PartitionSpec as P

CORES = 2
EPS = 1e-05
BLOCK = 128
LIMIT = 8 * 2**20
BESIDE = 10**10


def normalize(x, gain):
    xf = x.astype(jnp.float32)
    return (xf * lax.rsqrt(jnp.mean(xf * xf, axis=-1, keepdims=True) + EPS) * gain).astype(jnp.bfloat16)


def role_at(tick):
    return (lax.axis_index("pipe") + lax.axis_index("zero") % CORES + tick + 1) % 2


def group_kernel(tick, other, ready, count, chips, mark_ref, gains_ref, gate_ref, up_ref, down_ref, *refs):
    group = (role_at(tick) + other) % 2
    pieces, outs = refs[:count], refs[count:]
    normed = jnp.concatenate([ref[...] for ref in pieces], axis=0)
    if not ready:
        normed = normalize(normed, gains_ref[pl.ds(group, 1), :])
    hidden = []
    for first in range(0, gate_ref.shape[2], BLOCK):
        block = pl.ds(first, BLOCK)
        gate = jnp.dot(normed, gate_ref[group, :, block], preferred_element_type=jnp.float32)
        up = jnp.dot(normed, up_ref[group, :, block], preferred_element_type=jnp.float32)
        hidden.append((gate / (1.0 + jnp.exp(-gate)) * up).astype(jnp.bfloat16))
    hidden = jnp.concatenate(hidden, axis=1)
    first_core = lax.axis_index("zero") % CORES == 0
    for first in range(0, down_ref.shape[2], BLOCK):
        block = pl.ds(first, BLOCK)
        part = jnp.dot(hidden, down_ref[group, :, block], preferred_element_type=jnp.float32)
        if len(outs) == 1:
            outs[0][:, block] = part.astype(outs[0].dtype)
            continue
        rows = part.shape[0] // (CORES * chips)
        halves = [part[n * rows : (n + 1) * rows] for n in range(CORES * chips)]
        keep = [jnp.where(first_core, a, b) for a, b in zip(halves[::2], halves[1::2])]
        give = [jnp.where(first_core, b, a) for a, b in zip(halves[::2], halves[1::2])]
        outs[0][:, block] = jnp.concatenate(keep, axis=0).astype(outs[0].dtype)
        outs[1][:, block] = jnp.concatenate(give, axis=0).astype(outs[1].dtype)


def pass_kernel(x_ref, out):
    out[...] = x_ref[...]


def passed(x):
    vmem = pl.BlockSpec(memory_space=pltpu.VMEM)
    return pl.pallas_call(
        pass_kernel,
        out_shape=jax.ShapeDtypeStruct(x.shape, x.dtype),
        in_specs=[vmem],
        out_specs=vmem,
        compiler_params=pltpu.CompilerParams(vmem_limit_bytes=LIMIT),
        cost_estimate=pl.CostEstimate(flops=BESIDE, bytes_accessed=4 * x.size, transcendentals=0),
    )(x)


def stack_kernel(mark_ref, *refs):
    height = refs[0].shape[0]
    for slot, ref in enumerate(refs[:-1]):
        refs[-1][slot * height : (slot + 1) * height] = ref[...]


def stacked(pieces, mark):
    vmem = pl.BlockSpec(memory_space=pltpu.VMEM)
    rows, width = pieces[0].shape
    return pl.pallas_call(
        stack_kernel,
        out_shape=jax.ShapeDtypeStruct((len(pieces) * rows, width), pieces[0].dtype),
        in_specs=[vmem] * (1 + len(pieces)),
        out_specs=vmem,
        compiler_params=pltpu.CompilerParams(vmem_limit_bytes=LIMIT),
    )(mark, *pieces)


def spread_kernel(slots, part_ref, got_ref, x_ref, *outs):
    height = x_ref.shape[0]
    for step, (slot, out) in enumerate(zip(slots, outs)):
        place = slice(slot * height, (slot + 1) * height)
        total = part_ref[place] + got_ref[place].astype(jnp.float32)
        if step == 0:
            total += x_ref[...].astype(jnp.float32)
        out[...] = total.astype(out.dtype)


def spread(slots, part, got, x):
    vmem = pl.BlockSpec(memory_space=pltpu.VMEM)
    return pl.pallas_call(
        functools.partial(spread_kernel, slots),
        out_shape=(jax.ShapeDtypeStruct(x.shape, x.dtype),) * len(slots),
        in_specs=[vmem] * 3,
        out_specs=(vmem,) * len(slots),
        compiler_params=pltpu.CompilerParams(vmem_limit_bytes=LIMIT),
    )(part, got, x)


def spread_rows_kernel(slots, mine_ref, theirs_ref, to_mine_ref, to_theirs_ref, here_ref, there_ref, *outs):
    rows = here_ref.shape[0]
    groups = (mine_ref, to_mine_ref, here_ref), (theirs_ref, to_theirs_ref, there_ref)
    for step, (slot, out) in enumerate(zip(slots, outs)):
        place = slice(slot * rows, (slot + 1) * rows)
        totals = [part[place] + got[place].astype(jnp.float32) for part, got, x in groups]
        if step == 0:
            totals = [total + x[...].astype(jnp.float32) for total, (part, got, x) in zip(totals, groups)]
        out[...] = jnp.concatenate(totals, axis=0).astype(out.dtype)


def spread_rows(slots, mine, theirs, to_mine, to_theirs, here, there):
    vmem = pl.BlockSpec(memory_space=pltpu.VMEM)
    rows, width = here.shape
    return pl.pallas_call(
        functools.partial(spread_rows_kernel, slots),
        out_shape=tuple(
            jax.ShapeDtypeStruct((2 * rows, width), jnp.float32 if step == 0 else here.dtype)
            for step in range(len(slots))
        ),
        in_specs=[vmem] * 6,
        out_specs=(vmem,) * len(slots),
        compiler_params=pltpu.CompilerParams(vmem_limit_bytes=LIMIT),
    )(mine, theirs, to_mine, to_theirs, here, there)


def sum_kernel(*refs):
    total = refs[0][...].astype(jnp.float32)
    for ref in refs[1:-1]:
        total += ref[...].astype(jnp.float32)
    refs[-1][...] = total.astype(refs[-1].dtype)


def summed(parts):
    vmem = pl.BlockSpec(memory_space=pltpu.VMEM)
    return pl.pallas_call(
        sum_kernel,
        out_shape=jax.ShapeDtypeStruct(parts[0].shape, jnp.bfloat16),
        in_specs=[vmem] * len(parts),
        out_specs=vmem,
        compiler_params=pltpu.CompilerParams(vmem_limit_bytes=LIMIT),
    )(*parts)


def next_kernel(tick, gains_ref, entering_ref, *refs):
    *parts, x_out, normed_out = refs
    total = parts[0][...].astype(jnp.float32)
    for part in parts[1:]:
        total += part[...].astype(jnp.float32)
    role = role_at(tick)
    entry = (lax.axis_index("pipe") == 0) & (role == 0)
    x = jnp.where(entry, entering_ref[...].astype(jnp.float32), total).astype(x_out.dtype)
    x_out[...] = x
    normed_out[...] = normalize(x, gains_ref[pl.ds(role, 1), :])


def next_rows(tick, gains, entering, parts):
    vmem = pl.BlockSpec(memory_space=pltpu.VMEM)
    shape = jax.ShapeDtypeStruct(entering.shape, entering.dtype)
    return pl.pallas_call(
        functools.partial(next_kernel, tick),
        out_shape=(shape, shape),
        in_specs=[vmem] * (2 + len(parts)),
        out_specs=(vmem, vmem),
        compiler_params=pltpu.CompilerParams(vmem_limit_bytes=LIMIT),
    )(gains, entering, *parts)


def partial(tick, other, ready, split, chips, pieces, gains, weights, mark):
    vmem = pl.BlockSpec(memory_space=pltpu.VMEM)
    rows, width = sum(piece.shape[0] for piece in pieces), pieces[0].shape[1]
    size = sum(w.size // w.shape[0] for w in weights)
    out = jax.ShapeDtypeStruct((rows, width), jnp.bfloat16 if other else jnp.float32)
    if split:
        out = tuple(jax.ShapeDtypeStruct((rows // CORES, width), dtype) for dtype in (jnp.float32, jnp.bfloat16))
    return pl.pallas_call(
        functools.partial(group_kernel, tick, other, ready, len(pieces), chips),
        out_shape=out,
        in_specs=[vmem] * (2 + len(weights) + len(pieces)),
        out_specs=(vmem, vmem) if split else vmem,
        compiler_params=pltpu.CompilerParams(vmem_limit_bytes=LIMIT),
        cost_estimate=pl.CostEstimate(flops=2 * rows * size, bytes_accessed=2 * size, transcendentals=0),
    )(mark, gains, *weights, *pieces)


def chip_pairs(chips, step):
    if chips & (chips - 1) == 0:
        return [(chip, chip ^ step) for chip in range(chips)]
    return [(chip, (chip + step) % chips) for chip in range(chips)]


def on_device(down_out, up_out, feeds, order, gains, gate_w, up_w, down_w):
    sections, zero = lax.axis_size("pipe"), lax.axis_size("zero")
    chips = zero // CORES
    section, place = lax.axis_index("pipe"), lax.axis_index("zero")
    core = place % CORES
    ticks = feeds.shape[0]
    both = ("pipe", "zero")

    def to_sibling(value):
        return lax.ppermute(value, "zero", [(k, k ^ 1) for k in range(zero)])

    def to_chip(value, step):
        pairs = [(a * CORES + r, b * CORES + r) for a, b in chip_pairs(chips, step) for r in range(CORES)]
        return lax.ppermute(value, "zero", pairs)

    def to_next(value, tick, step):
        pairs = []
        for s in range(sections):
            for r in range(CORES):
                other = s - 1 if (s + r + tick + 1) % 2 == 0 else s + 1
                other = other if 0 <= other < sections else s
                for a, b in chip_pairs(chips, step):
                    pairs.append((s * zero + a * CORES + r, other * zero + b * CORES + r))
        return lax.ppermute(value, both, pairs)

    def joined(own, other):
        first = jnp.where(core == 0, own, other)
        second = jnp.where(core == 0, other, own)
        return jnp.concatenate([first, second], axis=0)

    weights = (gate_w[0], up_w[0], down_w[0])
    place_in_pipe = jnp.full((1, ticks), section, jnp.float32)
    numbers = jnp.arange(ticks) + (passed(place_in_pipe)[0] - place_in_pipe[0]).astype(order.dtype)
    chosen = (order[:, None] == numbers[None, :]).astype(feeds.dtype)
    fed = jnp.einsum("tn,nrd->trd", chosen, feeds, preferred_element_type=jnp.float32).astype(feeds.dtype)
    was_down = role_at(1) == 0
    ascended = jnp.where(section == 0, fed[0], up_out[0])
    given = jnp.where(was_down, ascended, down_out[0])
    own = jnp.where(was_down, down_out[0], ascended)
    rows = own.shape[0]
    given = jnp.concatenate([given] + [fed[tick] for tick in range(1, ticks)], axis=0)
    own, given = lax.optimization_barrier((own, given))
    taken = to_sibling(given)
    state = joined(own, taken[:rows])
    entering = [joined(given[rows * tick : rows * (tick + 1)], taken[rows * tick : rows * (tick + 1)]) for tick in range(1, ticks)]

    for tick in range(ticks):
        if tick == 0:
            pieces = [to_next(state, tick, step) for step in range(chips)]
        else:
            pieces = [normed] + [to_chip(normed, step) for step in range(1, chips)]
        x = pieces[0] if tick == 0 else state
        height = x.shape[0]
        mark = passed(state)
        pieces = pieces[::-1]
        slots = [step if chips & (chips - 1) == 0 else (chips - step) % chips for step in range(chips)]
        slots = [chips - 1 - slot for slot in slots]
        if tick + 1 == ticks:
            break
        siblings = [to_sibling(piece) for piece in pieces]
        part = partial(tick, 0, tick > 0, False, chips, pieces, gains[0], weights, mark)
        given = partial(tick, 1, tick > 0, False, chips, siblings, gains[0], weights, mark)
        sums = spread(slots, part, to_sibling(given), x)
        sums = [to_next(part, tick + 1, step) for step, part in enumerate(sums)]
        state, normed = next_rows(tick + 1, gains[0], entering[tick], sums[::-1])

    rows_here = jnp.where(core == 0, x[:rows], x[rows:])
    rows_there = to_sibling(jnp.where(core == 0, x[rows:], x[:rows]))
    stack = stacked(pieces, rows_there)
    mine, given = partial(tick, 0, tick > 0, True, chips, [stack], gains[0], weights, mark)
    theirs, back = partial(tick, 1, tick > 0, True, chips, [to_sibling(stack)], gains[0], weights, mark)
    sums = list(spread_rows(slots, mine, theirs, to_sibling(back), to_sibling(given), rows_here, rows_there))
    sums[1:] = [to_chip(part, step) for step, part in enumerate(sums) if step > 0]
    state = summed(sums[::-1])
    role = role_at(ticks - 1)
    down_state = jnp.where(role == 0, state[:rows], state[rows:])
    up_state = jnp.where(role == 0, state[rows:], state[:rows])
    return (down_state[None], up_state[None])


def solution(mesh):
    return jax.shard_map(
        on_device,
        mesh=mesh,
        in_specs=(
            P("pipe", "zero", None),
            P("pipe", "zero", None),
            P(None, "zero", None),
            P(),
            P("pipe", None, None),
            P("pipe", None, None, "zero"),
            P("pipe", None, None, "zero"),
            P("pipe", None, "zero", None),
        ),
        out_specs=(P("pipe", "zero", None), P("pipe", "zero", None)),
        check_vma=False,
    )
```

```python
import functools

import jax
import jax.numpy as jnp
from jax import lax
from jax.experimental import pallas as pl
from jax.experimental.pallas import tpu as pltpu
from jax.sharding import PartitionSpec as P

CORES = 2
EPS = 1e-05
BLOCK = 128
LIMIT = 8 * 2**20
BESIDE = 10**10


def normalize(x, gain):
    xf = x.astype(jnp.float32)
    return (xf * lax.rsqrt(jnp.mean(xf * xf, axis=-1, keepdims=True) + EPS) * gain).astype(jnp.bfloat16)


def role_at(tick):
    return (lax.axis_index("pipe") + lax.axis_index("zero") % CORES + tick + 1) % 2


def group_kernel(tick, other, ready, count, chips, mark_ref, gains_ref, gate_ref, up_ref, down_ref, *refs):
    group = (role_at(tick) + other) % 2
    pieces, outs = refs[:count], refs[count:]
    normed = jnp.concatenate([ref[...] for ref in pieces], axis=0)
    if not ready:
        normed = normalize(normed, gains_ref[pl.ds(group, 1), :])
    hidden = []
    for first in range(0, gate_ref.shape[2], BLOCK):
        block = pl.ds(first, BLOCK)
        gate = jnp.dot(normed, gate_ref[group, :, block], preferred_element_type=jnp.float32)
        up = jnp.dot(normed, up_ref[group, :, block], preferred_element_type=jnp.float32)
        hidden.append((gate / (1.0 + jnp.exp(-gate)) * up).astype(jnp.bfloat16))
    hidden = jnp.concatenate(hidden, axis=1)
    first_core = lax.axis_index("zero") % CORES == 0
    for first in range(0, down_ref.shape[2], BLOCK):
        block = pl.ds(first, BLOCK)
        part = jnp.dot(hidden, down_ref[group, :, block], preferred_element_type=jnp.float32)
        if len(outs) == 1:
            outs[0][:, block] = part.astype(outs[0].dtype)
            continue
        rows = part.shape[0] // (CORES * chips)
        halves = [part[n * rows : (n + 1) * rows] for n in range(CORES * chips)]
        keep = [jnp.where(first_core, a, b) for a, b in zip(halves[::2], halves[1::2])]
        give = [jnp.where(first_core, b, a) for a, b in zip(halves[::2], halves[1::2])]
        outs[0][:, block] = jnp.concatenate(keep, axis=0).astype(outs[0].dtype)
        outs[1][:, block] = jnp.concatenate(give, axis=0).astype(outs[1].dtype)


def pass_kernel(x_ref, out):
    out[...] = x_ref[...]


def passed(x):
    vmem = pl.BlockSpec(memory_space=pltpu.VMEM)
    return pl.pallas_call(
        pass_kernel,
        out_shape=jax.ShapeDtypeStruct(x.shape, x.dtype),
        in_specs=[vmem],
        out_specs=vmem,
        compiler_params=pltpu.CompilerParams(vmem_limit_bytes=LIMIT),
        cost_estimate=pl.CostEstimate(flops=BESIDE, bytes_accessed=4 * x.size, transcendentals=0),
    )(x)


def stack_kernel(mark_ref, *refs):
    height = refs[0].shape[0]
    for slot, ref in enumerate(refs[:-1]):
        refs[-1][slot * height : (slot + 1) * height] = ref[...]


def stacked(pieces, mark):
    vmem = pl.BlockSpec(memory_space=pltpu.VMEM)
    rows, width = pieces[0].shape
    return pl.pallas_call(
        stack_kernel,
        out_shape=jax.ShapeDtypeStruct((len(pieces) * rows, width), pieces[0].dtype),
        in_specs=[vmem] * (1 + len(pieces)),
        out_specs=vmem,
        compiler_params=pltpu.CompilerParams(vmem_limit_bytes=LIMIT),
    )(mark, *pieces)


def spread_kernel(slots, part_ref, got_ref, x_ref, *outs):
    height = x_ref.shape[0]
    for step, (slot, out) in enumerate(zip(slots, outs)):
        place = slice(slot * height, (slot + 1) * height)
        total = part_ref[place] + got_ref[place].astype(jnp.float32)
        if step == 0:
            total += x_ref[...].astype(jnp.float32)
        out[...] = total.astype(out.dtype)


def spread(slots, part, got, x):
    vmem = pl.BlockSpec(memory_space=pltpu.VMEM)
    return pl.pallas_call(
        functools.partial(spread_kernel, slots),
        out_shape=(jax.ShapeDtypeStruct(x.shape, x.dtype),) * len(slots),
        in_specs=[vmem] * 3,
        out_specs=(vmem,) * len(slots),
        compiler_params=pltpu.CompilerParams(vmem_limit_bytes=LIMIT),
    )(part, got, x)


def spread_rows_kernel(slots, mine_ref, theirs_ref, to_mine_ref, to_theirs_ref, here_ref, there_ref, *outs):
    rows = here_ref.shape[0]
    groups = (mine_ref, to_mine_ref, here_ref), (theirs_ref, to_theirs_ref, there_ref)
    for step, (slot, out) in enumerate(zip(slots, outs)):
        place = slice(slot * rows, (slot + 1) * rows)
        totals = [part[place] + got[place].astype(jnp.float32) for part, got, x in groups]
        if step == 0:
            totals = [total + x[...].astype(jnp.float32) for total, (part, got, x) in zip(totals, groups)]
        out[...] = jnp.concatenate(totals, axis=0).astype(out.dtype)


def spread_rows(slots, mine, theirs, to_mine, to_theirs, here, there):
    vmem = pl.BlockSpec(memory_space=pltpu.VMEM)
    rows, width = here.shape
    return pl.pallas_call(
        functools.partial(spread_rows_kernel, slots),
        out_shape=tuple(
            jax.ShapeDtypeStruct((2 * rows, width), jnp.float32 if step == 0 else here.dtype)
            for step in range(len(slots))
        ),
        in_specs=[vmem] * 6,
        out_specs=(vmem,) * len(slots),
        compiler_params=pltpu.CompilerParams(vmem_limit_bytes=LIMIT),
    )(mine, theirs, to_mine, to_theirs, here, there)


def sum_kernel(*refs):
    total = refs[0][...].astype(jnp.float32)
    for ref in refs[1:-1]:
        total += ref[...].astype(jnp.float32)
    refs[-1][...] = total.astype(refs[-1].dtype)


def summed(parts):
    vmem = pl.BlockSpec(memory_space=pltpu.VMEM)
    return pl.pallas_call(
        sum_kernel,
        out_shape=jax.ShapeDtypeStruct(parts[0].shape, jnp.bfloat16),
        in_specs=[vmem] * len(parts),
        out_specs=vmem,
        compiler_params=pltpu.CompilerParams(vmem_limit_bytes=LIMIT),
    )(*parts)


def next_kernel(tick, gains_ref, entering_ref, *refs):
    *parts, x_out, normed_out = refs
    total = parts[0][...].astype(jnp.float32)
    for part in parts[1:]:
        total += part[...].astype(jnp.float32)
    role = role_at(tick)
    entry = (lax.axis_index("pipe") == 0) & (role == 0)
    x = jnp.where(entry, entering_ref[...].astype(jnp.float32), total).astype(x_out.dtype)
    x_out[...] = x
    normed_out[...] = normalize(x, gains_ref[pl.ds(role, 1), :])


def next_rows(tick, gains, entering, parts):
    vmem = pl.BlockSpec(memory_space=pltpu.VMEM)
    shape = jax.ShapeDtypeStruct(entering.shape, entering.dtype)
    return pl.pallas_call(
        functools.partial(next_kernel, tick),
        out_shape=(shape, shape),
        in_specs=[vmem] * (2 + len(parts)),
        out_specs=(vmem, vmem),
        compiler_params=pltpu.CompilerParams(vmem_limit_bytes=LIMIT),
    )(gains, entering, *parts)


def partial(tick, other, ready, split, chips, pieces, gains, weights, mark):
    vmem = pl.BlockSpec(memory_space=pltpu.VMEM)
    rows, width = sum(piece.shape[0] for piece in pieces), pieces[0].shape[1]
    size = sum(w.size // w.shape[0] for w in weights)
    out = jax.ShapeDtypeStruct((rows, width), jnp.bfloat16 if other else jnp.float32)
    if split:
        out = tuple(jax.ShapeDtypeStruct((rows // CORES, width), dtype) for dtype in (jnp.float32, jnp.bfloat16))
    return pl.pallas_call(
        functools.partial(group_kernel, tick, other, ready, len(pieces), chips),
        out_shape=out,
        in_specs=[vmem] * (2 + len(weights) + len(pieces)),
        out_specs=(vmem, vmem) if split else vmem,
        compiler_params=pltpu.CompilerParams(vmem_limit_bytes=LIMIT),
        cost_estimate=pl.CostEstimate(flops=2 * rows * size, bytes_accessed=2 * size, transcendentals=0),
    )(mark, gains, *weights, *pieces)


def chip_pairs(chips, step):
    if chips & (chips - 1) == 0:
        return [(chip, chip ^ step) for chip in range(chips)]
    return [(chip, (chip + step) % chips) for chip in range(chips)]


def on_device(down_out, up_out, feeds, order, gains, gate_w, up_w, down_w):
    sections, zero = lax.axis_size("pipe"), lax.axis_size("zero")
    chips = zero // CORES
    section, place = lax.axis_index("pipe"), lax.axis_index("zero")
    core = place % CORES
    ticks = feeds.shape[0]
    both = ("pipe", "zero")

    def to_sibling(value):
        return lax.ppermute(value, "zero", [(k, k ^ 1) for k in range(zero)])

    def to_chip(value, step):
        pairs = [(a * CORES + r, b * CORES + r) for a, b in chip_pairs(chips, step) for r in range(CORES)]
        return lax.ppermute(value, "zero", pairs)

    def to_next(value, tick, step):
        pairs = []
        for s in range(sections):
            for r in range(CORES):
                other = s - 1 if (s + r + tick + 1) % 2 == 0 else s + 1
                other = other if 0 <= other < sections else s
                for a, b in chip_pairs(chips, step):
                    pairs.append((s * zero + a * CORES + r, other * zero + b * CORES + r))
        return lax.ppermute(value, both, pairs)

    def joined(own, other):
        first = jnp.where(core == 0, own, other)
        second = jnp.where(core == 0, other, own)
        return jnp.concatenate([first, second], axis=0)

    weights = (gate_w[0], up_w[0], down_w[0])
    place_in_pipe = jnp.full((1, ticks), section, jnp.float32)
    numbers = jnp.arange(ticks) + (passed(place_in_pipe)[0] - place_in_pipe[0]).astype(order.dtype)
    chosen = (order[:, None] == numbers[None, :]).astype(feeds.dtype)
    fed = jnp.einsum("tn,nrd->trd", chosen, feeds, preferred_element_type=jnp.float32).astype(feeds.dtype)
    was_down = role_at(1) == 0
    ascended = jnp.where(section == 0, fed[0], up_out[0])
    given = jnp.where(was_down, ascended, down_out[0])
    own = jnp.where(was_down, down_out[0], ascended)
    rows = own.shape[0]
    own, given, later = lax.optimization_barrier((own, given, [fed[tick] for tick in range(1, ticks)]))
    state = joined(own, to_sibling(given))
    entering = [joined(feed, to_sibling(feed)) for feed in later]

    for tick in range(ticks):
        if tick == 0:
            pieces = [to_next(state, tick, step) for step in range(chips)]
        else:
            pieces = [normed] + [to_chip(normed, step) for step in range(1, chips)]
        x = pieces[0] if tick == 0 else state
        height = x.shape[0]
        mark = passed(state)
        pieces = pieces[::-1]
        slots = [step if chips & (chips - 1) == 0 else (chips - step) % chips for step in range(chips)]
        slots = [chips - 1 - slot for slot in slots]
        if tick + 1 == ticks:
            break
        siblings = [to_sibling(piece) for piece in pieces]
        part = partial(tick, 0, tick > 0, False, chips, pieces, gains[0], weights, mark)
        given = partial(tick, 1, tick > 0, False, chips, siblings, gains[0], weights, mark)
        sums = spread(slots, part, to_sibling(given), x)
        sums = [to_next(part, tick + 1, step) for step, part in enumerate(sums)]
        state, normed = next_rows(tick + 1, gains[0], entering[tick], sums[::-1])

    rows_here = jnp.where(core == 0, x[:rows], x[rows:])
    rows_there = to_sibling(jnp.where(core == 0, x[rows:], x[:rows]))
    stack = stacked(pieces, rows_there)
    mine, given = partial(tick, 0, tick > 0, True, chips, [stack], gains[0], weights, mark)
    theirs, back = partial(tick, 1, tick > 0, True, chips, [to_sibling(stack)], gains[0], weights, mark)
    sums = list(spread_rows(slots, mine, theirs, to_sibling(back), to_sibling(given), rows_here, rows_there))
    sums[1:] = [to_chip(part, step) for step, part in enumerate(sums) if step > 0]
    state = summed(sums[::-1])
    role = role_at(ticks - 1)
    down_state = jnp.where(role == 0, state[:rows], state[rows:])
    up_state = jnp.where(role == 0, state[rows:], state[:rows])
    return (down_state[None], up_state[None])


def solution(mesh):
    return jax.shard_map(
        on_device,
        mesh=mesh,
        in_specs=(
            P("pipe", "zero", None),
            P("pipe", "zero", None),
            P(None, "zero", None),
            P(),
            P("pipe", None, None),
            P("pipe", None, None, "zero"),
            P("pipe", None, None, "zero"),
            P("pipe", None, "zero", None),
        ),
        out_specs=(P("pipe", "zero", None), P("pipe", "zero", None)),
        check_vma=False,
    )
```

```python
import functools

import jax
import jax.numpy as jnp
from jax import lax
from jax.experimental import pallas as pl
from jax.experimental.pallas import tpu as pltpu
from jax.sharding import PartitionSpec as P

CORES = 2
EPS = 1e-05
BLOCK = 128
LIMIT = 8 * 2**20
BESIDE = 10**10


def normalize(x, gain):
    xf = x.astype(jnp.float32)
    return (xf * lax.rsqrt(jnp.mean(xf * xf, axis=-1, keepdims=True) + EPS) * gain).astype(jnp.bfloat16)


def role_at(tick):
    return (lax.axis_index("pipe") + lax.axis_index("zero") % CORES + tick + 1) % 2


def group_kernel(tick, other, ready, count, chips, mark_ref, gains_ref, gate_ref, up_ref, down_ref, *refs):
    group = (role_at(tick) + other) % 2
    pieces, outs = refs[:count], refs[count:]
    normed = jnp.concatenate([ref[...] for ref in pieces], axis=0)
    if not ready:
        normed = normalize(normed, gains_ref[pl.ds(group, 1), :])
    hidden = []
    for first in range(0, gate_ref.shape[2], BLOCK):
        block = pl.ds(first, BLOCK)
        gate = jnp.dot(normed, gate_ref[group, :, block], preferred_element_type=jnp.float32)
        up = jnp.dot(normed, up_ref[group, :, block], preferred_element_type=jnp.float32)
        hidden.append((gate / (1.0 + jnp.exp(-gate)) * up).astype(jnp.bfloat16))
    hidden = jnp.concatenate(hidden, axis=1)
    first_core = lax.axis_index("zero") % CORES == 0
    for first in range(0, down_ref.shape[2], BLOCK):
        block = pl.ds(first, BLOCK)
        part = jnp.dot(hidden, down_ref[group, :, block], preferred_element_type=jnp.float32)
        if len(outs) == 1:
            outs[0][:, block] = part.astype(outs[0].dtype)
            continue
        rows = part.shape[0] // (CORES * chips)
        halves = [part[n * rows : (n + 1) * rows] for n in range(CORES * chips)]
        keep = [jnp.where(first_core, a, b) for a, b in zip(halves[::2], halves[1::2])]
        give = [jnp.where(first_core, b, a) for a, b in zip(halves[::2], halves[1::2])]
        outs[0][:, block] = jnp.concatenate(keep, axis=0).astype(outs[0].dtype)
        outs[1][:, block] = jnp.concatenate(give, axis=0).astype(outs[1].dtype)


def pass_kernel(x_ref, out):
    out[...] = x_ref[...]


def passed(x):
    vmem = pl.BlockSpec(memory_space=pltpu.VMEM)
    return pl.pallas_call(
        pass_kernel,
        out_shape=jax.ShapeDtypeStruct(x.shape, x.dtype),
        in_specs=[vmem],
        out_specs=vmem,
        compiler_params=pltpu.CompilerParams(vmem_limit_bytes=LIMIT),
        cost_estimate=pl.CostEstimate(flops=BESIDE, bytes_accessed=4 * x.size, transcendentals=0),
    )(x)


def stack_kernel(mark_ref, *refs):
    height = refs[0].shape[0]
    for slot, ref in enumerate(refs[:-1]):
        refs[-1][slot * height : (slot + 1) * height] = ref[...]


def stacked(pieces, mark):
    vmem = pl.BlockSpec(memory_space=pltpu.VMEM)
    rows, width = pieces[0].shape
    return pl.pallas_call(
        stack_kernel,
        out_shape=jax.ShapeDtypeStruct((len(pieces) * rows, width), pieces[0].dtype),
        in_specs=[vmem] * (1 + len(pieces)),
        out_specs=vmem,
        compiler_params=pltpu.CompilerParams(vmem_limit_bytes=LIMIT),
    )(mark, *pieces)


def spread_kernel(slots, part_ref, got_ref, x_ref, *outs):
    height = x_ref.shape[0]
    for step, (slot, out) in enumerate(zip(slots, outs)):
        place = slice(slot * height, (slot + 1) * height)
        total = part_ref[place] + got_ref[place].astype(jnp.float32)
        if step == 0:
            total += x_ref[...].astype(jnp.float32)
        out[...] = total.astype(out.dtype)


def spread(slots, part, got, x):
    vmem = pl.BlockSpec(memory_space=pltpu.VMEM)
    return pl.pallas_call(
        functools.partial(spread_kernel, slots),
        out_shape=(jax.ShapeDtypeStruct(x.shape, x.dtype),) * len(slots),
        in_specs=[vmem] * 3,
        out_specs=(vmem,) * len(slots),
        compiler_params=pltpu.CompilerParams(vmem_limit_bytes=LIMIT),
    )(part, got, x)


def spread_rows_kernel(slots, mine_ref, theirs_ref, to_mine_ref, to_theirs_ref, here_ref, there_ref, *outs):
    rows = here_ref.shape[0]
    groups = (mine_ref, to_mine_ref, here_ref), (theirs_ref, to_theirs_ref, there_ref)
    for step, (slot, out) in enumerate(zip(slots, outs)):
        place = slice(slot * rows, (slot + 1) * rows)
        totals = [part[place] + got[place].astype(jnp.float32) for part, got, x in groups]
        if step == 0:
            totals = [total + x[...].astype(jnp.float32) for total, (part, got, x) in zip(totals, groups)]
        out[...] = jnp.concatenate(totals, axis=0).astype(out.dtype)


def spread_rows(slots, mine, theirs, to_mine, to_theirs, here, there):
    vmem = pl.BlockSpec(memory_space=pltpu.VMEM)
    rows, width = here.shape
    return pl.pallas_call(
        functools.partial(spread_rows_kernel, slots),
        out_shape=tuple(
            jax.ShapeDtypeStruct((2 * rows, width), jnp.float32 if step == 0 else here.dtype)
            for step in range(len(slots))
        ),
        in_specs=[vmem] * 6,
        out_specs=(vmem,) * len(slots),
        compiler_params=pltpu.CompilerParams(vmem_limit_bytes=LIMIT),
    )(mine, theirs, to_mine, to_theirs, here, there)


def sum_kernel(*refs):
    total = refs[0][...].astype(jnp.float32)
    for ref in refs[1:-1]:
        total += ref[...].astype(jnp.float32)
    refs[-1][...] = total.astype(refs[-1].dtype)


def summed(parts):
    vmem = pl.BlockSpec(memory_space=pltpu.VMEM)
    return pl.pallas_call(
        sum_kernel,
        out_shape=jax.ShapeDtypeStruct(parts[0].shape, jnp.bfloat16),
        in_specs=[vmem] * len(parts),
        out_specs=vmem,
        compiler_params=pltpu.CompilerParams(vmem_limit_bytes=LIMIT),
    )(*parts)


def next_kernel(tick, gains_ref, entering_ref, *refs):
    *parts, x_out, normed_out = refs
    total = parts[0][...].astype(jnp.float32)
    for part in parts[1:]:
        total += part[...].astype(jnp.float32)
    role = role_at(tick)
    entry = (lax.axis_index("pipe") == 0) & (role == 0)
    x = jnp.where(entry, entering_ref[...].astype(jnp.float32), total).astype(x_out.dtype)
    x_out[...] = x
    normed_out[...] = normalize(x, gains_ref[pl.ds(role, 1), :])


def next_rows(tick, gains, entering, parts):
    vmem = pl.BlockSpec(memory_space=pltpu.VMEM)
    shape = jax.ShapeDtypeStruct(entering.shape, entering.dtype)
    return pl.pallas_call(
        functools.partial(next_kernel, tick),
        out_shape=(shape, shape),
        in_specs=[vmem] * (2 + len(parts)),
        out_specs=(vmem, vmem),
        compiler_params=pltpu.CompilerParams(vmem_limit_bytes=LIMIT),
    )(gains, entering, *parts)


def partial(tick, other, ready, split, chips, pieces, gains, weights, mark):
    vmem = pl.BlockSpec(memory_space=pltpu.VMEM)
    rows, width = sum(piece.shape[0] for piece in pieces), pieces[0].shape[1]
    size = sum(w.size // w.shape[0] for w in weights)
    out = jax.ShapeDtypeStruct((rows, width), jnp.bfloat16 if other else jnp.float32)
    if split:
        out = tuple(jax.ShapeDtypeStruct((rows // CORES, width), dtype) for dtype in (jnp.float32, jnp.bfloat16))
    return pl.pallas_call(
        functools.partial(group_kernel, tick, other, ready, len(pieces), chips),
        out_shape=out,
        in_specs=[vmem] * (2 + len(weights) + len(pieces)),
        out_specs=(vmem, vmem) if split else vmem,
        compiler_params=pltpu.CompilerParams(vmem_limit_bytes=LIMIT),
        cost_estimate=pl.CostEstimate(flops=2 * rows * size, bytes_accessed=2 * size, transcendentals=0),
    )(mark, gains, *weights, *pieces)


def chip_pairs(chips, step):
    if chips & (chips - 1) == 0:
        return [(chip, chip ^ step) for chip in range(chips)]
    return [(chip, (chip + step) % chips) for chip in range(chips)]


def on_device(down_out, up_out, feeds, order, gains, gate_w, up_w, down_w):
    sections, zero = lax.axis_size("pipe"), lax.axis_size("zero")
    chips = zero // CORES
    section, place = lax.axis_index("pipe"), lax.axis_index("zero")
    core = place % CORES
    ticks = feeds.shape[0]
    both = ("pipe", "zero")

    def to_sibling(value):
        return lax.ppermute(value, "zero", [(k, k ^ 1) for k in range(zero)])

    def to_chip(value, step):
        pairs = [(a * CORES + r, b * CORES + r) for a, b in chip_pairs(chips, step) for r in range(CORES)]
        return lax.ppermute(value, "zero", pairs)

    def to_next(value, tick, step):
        pairs = []
        for s in range(sections):
            for r in range(CORES):
                other = s - 1 if (s + r + tick + 1) % 2 == 0 else s + 1
                other = other if 0 <= other < sections else s
                for a, b in chip_pairs(chips, step):
                    pairs.append((s * zero + a * CORES + r, other * zero + b * CORES + r))
        return lax.ppermute(value, both, pairs)

    def joined(own, other):
        first = jnp.where(core == 0, own, other)
        second = jnp.where(core == 0, other, own)
        return jnp.concatenate([first, second], axis=0)

    weights = (gate_w[0], up_w[0], down_w[0])
    place_in_pipe = jnp.full((1, ticks), section, jnp.float32)
    numbers = jnp.arange(ticks) + (passed(place_in_pipe)[0] - place_in_pipe[0]).astype(order.dtype)
    chosen = (order[:, None] == numbers[None, :]).astype(feeds.dtype)
    fed = jnp.einsum("tn,nrd->trd", chosen, feeds, preferred_element_type=jnp.float32).astype(feeds.dtype)
    was_down = role_at(1) == 0
    ascended = jnp.where(section == 0, fed[0], up_out[0])
    given = jnp.where(was_down, ascended, down_out[0])
    own = jnp.where(was_down, down_out[0], ascended)
    rows = own.shape[0]
    own, given, later = lax.optimization_barrier((own, given, [fed[tick] for tick in range(1, ticks)]))
    state = joined(own, to_sibling(given))
    entering = [joined(feed, to_sibling(feed)) for feed in later]

    for tick in range(ticks):
        if tick == 0:
            pieces = [to_next(state, tick, step) for step in range(chips)]
        else:
            pieces = [normed] + [to_chip(normed, step) for step in range(1, chips)]
        x = pieces[0] if tick == 0 else state
        height = x.shape[0]
        mark = passed(state) if tick + 1 < ticks else gains[0]
        pieces = pieces[::-1]
        slots = [step if chips & (chips - 1) == 0 else (chips - step) % chips for step in range(chips)]
        slots = [chips - 1 - slot for slot in slots]
        if tick + 1 == ticks:
            break
        siblings = [to_sibling(piece) for piece in pieces]
        part = partial(tick, 0, tick > 0, False, chips, pieces, gains[0], weights, mark)
        given = partial(tick, 1, tick > 0, False, chips, siblings, gains[0], weights, mark)
        sums = spread(slots, part, to_sibling(given), x)
        sums = [to_next(part, tick + 1, step) for step, part in enumerate(sums)]
        state, normed = next_rows(tick + 1, gains[0], entering[tick], sums[::-1])

    rows_here = jnp.where(core == 0, x[:rows], x[rows:])
    rows_there = to_sibling(jnp.where(core == 0, x[rows:], x[:rows]))
    stack = stacked(pieces, rows_there)
    mine, given = partial(tick, 0, tick > 0, True, chips, [stack], gains[0], weights, mark)
    theirs, back = partial(tick, 1, tick > 0, True, chips, [to_sibling(stack)], gains[0], weights, mark)
    sums = list(spread_rows(slots, mine, theirs, to_sibling(back), to_sibling(given), rows_here, rows_there))
    sums[1:] = [to_chip(part, step) for step, part in enumerate(sums) if step > 0]
    state = summed(sums[::-1])
    role = role_at(ticks - 1)
    down_state = jnp.where(role == 0, state[:rows], state[rows:])
    up_state = jnp.where(role == 0, state[rows:], state[:rows])
    return (down_state[None], up_state[None])


def solution(mesh):
    return jax.shard_map(
        on_device,
        mesh=mesh,
        in_specs=(
            P("pipe", "zero", None),
            P("pipe", "zero", None),
            P(None, "zero", None),
            P(),
            P("pipe", None, None),
            P("pipe", None, None, "zero"),
            P("pipe", None, None, "zero"),
            P("pipe", None, "zero", None),
        ),
        out_specs=(P("pipe", "zero", None), P("pipe", "zero", None)),
        check_vma=False,
    )
```
